32 devices in a mesh: replica: 2 (over y), section: 4 (over x, core), tensor: 4 (over z).
Axes of the slice: x: 2, y: 2, z: 4, core: 2. Of those that a mesh axis runs over, the one named last changes fastest.
Arguments:
- hidden_in: bfloat16 [256, 8192], P('replica', 'tensor'), may hold values from -6 to 6
- lengths: int32 [2], P('replica'), may hold values from 1 to 128, 160 in all
- norm_gain: float32 [4, 8192], P('section'), may hold values from 0.1 to 1.9
- q_tiles: bfloat16 [4, 8192, 4096], P('section', 'replica', 'tensor'), may hold values from -4 to 4
- q_scales: bfloat16 [4, 64, 32], P('section', 'replica', 'tensor'), as said below
- kv_tiles: bfloat16 [4, 8192, 2048], P('section', 'replica', 'tensor'), may hold values from -4 to 4
- kv_scales: bfloat16 [4, 64, 16], P('section', 'replica', 'tensor'), as said below
- out_weight: bfloat16 [4, 4096, 8192], P('section', 'tensor'), may hold values from -0.09375 to 0.09375
Outputs:
- layer_outputs: bfloat16 [4, 256, 8192], P('section', 'replica', 'tensor')
- key_values: bfloat16 [4, 256, 2048], P('section', 'replica', 'tensor')
The draws below stay inside these ranges and needn't reach their ends.
Inputs may be any that keep to these rules, and one draw needn't show every extreme that they name: `q_scales`: every tile scale is positive. `kv_scales`: every tile scale is positive.
All inputs are finite; a program needn't handle non-finite values. No bound on the sum of `lengths` on one device may be relied on, other than what follows from the above.
Results may differ from the reference program's by a relative error of at most 0.015.
Values may be sent and summed in bfloat16 or wider, within the bound.
No kernel may reach another device: no remote copies, remote signals or barrier semaphores. Data moves between devices by JAX's collectives and lax.ppermute only.
A program may use at most 192 MiB of HBM per device.

```python
import math
import jax
import jax.numpy as jnp
import numpy as np
from jax import lax

D = 8192
QHEADS = 32
KVHEADS = 8
HEAD = 128
BLOCK = 128
ROWS = 128
LAYERS = 4
TOTAL_ROWS = 256
N_REPLICA = 2
N_TENSOR = 4


def draw_q_scales(key, part):
    key = jax.random.fold_in(key, 11)
    shape = (LAYERS, D // BLOCK, QHEADS * HEAD // BLOCK)
    level = jax.random.uniform(key, shape, jnp.float32, jnp.log(0.4), jnp.log(2.5))
    scales = jnp.exp(level) * D ** (-0.5)
    return scales.astype(jnp.bfloat16)


def draw_kv_scales(key, part):
    key = jax.random.fold_in(key, 23)
    shape = (LAYERS, D // BLOCK, KVHEADS * 2 * HEAD // BLOCK)
    level = jax.random.uniform(key, shape, jnp.float32, jnp.log(0.4), jnp.log(2.5))
    scales = jnp.exp(level) * D ** (-0.5)
    return scales.astype(jnp.bfloat16)


def level_of(own_key, dims, shards, low, top_value):
    level = 1.0
    for dim, shards_of in shards:
        steps = jax.random.uniform(jax.random.fold_in(jax.random.fold_in(own_key, 6), dim), (shards_of,), jnp.float32, low / len(shards), top_value / len(shards))
        level = level * jnp.repeat(jnp.exp(steps), dims[dim] // shards_of).reshape((-1,) + (1,) * (len(dims) - 1 - dim))
    return level


def length_profile(count, total, bound, lean):
    weights = [(1 << 20) // math.isqrt(grade ** lean) + 1 for grade in range(2, count + 1)]
    spare, counts = total - bound - (count - 1), [1] * (count - 1)
    while spare > 0:
        movable = [i for i in range(count - 1) if counts[i] < bound]
        whole, remaining = sum([weights[i] for i in movable]), spare
        for i in movable:
            more = min(bound - counts[i], max(1, remaining * weights[i] // whole), spare)
            counts[i] = counts[i] + more
            spare = spare - more
    return np.array([bound] + counts)


def uneven_parts(key, number_of, total, limit, skew):
    if number_of == 2:
        one = jax.random.randint(key, (), max(1, total - limit), min(limit, total - 1) + 1)
        return jnp.stack([one, total - one])
    tallies = jnp.asarray(length_profile(number_of, total, limit, skew), jnp.int32)
    twos = (number_of - 1) // 2
    donor, receiver = tallies[1:1 + 2 * twos:2], tallies[2:2 + 2 * twos:2]
    slack = jnp.minimum(donor - 1, limit - receiver)
    moved = jax.random.randint(jax.random.fold_in(key, 1), (twos,), 0, 1 << 20) % (slack + 1)
    tallies = tallies.at[1:1 + 2 * twos:2].set(donor - moved).at[2:2 + 2 * twos:2].set(receiver + moved)
    return tallies[jax.random.permutation(jax.random.fold_in(key, 2), number_of)]


def scatter_about(own_key, extent, scale, bound, pieces=(), kind=jnp.bfloat16):
    entries = scale * jax.random.normal(own_key, extent, jnp.float32)
    if pieces:
        entries = entries * level_of(own_key, extent, pieces, -0.22, 0.18)
    return jnp.clip(entries, -bound, bound).astype(kind)


def setup_inputs(seed: int = 0) -> dict:
    key_of = jax.random.split(jax.random.key(seed), 9)
    return {
        "hidden_in": scatter_about(key_of[0], (TOTAL_ROWS, D), 1.0, 6.0, ((0, 2), (1, 4))),
        "lengths": uneven_parts(key_of[1], N_REPLICA, N_REPLICA * ROWS * 5 // 8, ROWS, 1).astype(jnp.int32),
        "norm_gain": jnp.clip(1.0 + 0.18 * jax.random.normal(key_of[2], (LAYERS, D), jnp.float32), 0.1, 1.9),
        "q_tiles": scatter_about(key_of[3], (LAYERS, D, QHEADS * HEAD), 1.0, 4.0, ((0, 4), (1, 2), (2, 4))),
        "q_scales": draw_q_scales(jax.random.fold_in(key_of[8], 71), 0),
        "kv_tiles": scatter_about(key_of[5], (LAYERS, D, KVHEADS * 2 * HEAD), 1.0, 4.0, ((0, 4), (1, 2), (2, 4))),
        "kv_scales": draw_kv_scales(jax.random.fold_in(key_of[8], 71), 0),
        "out_weight": scatter_about(key_of[7], (LAYERS, QHEADS * HEAD, D), (QHEADS * HEAD) ** -0.5, 0.09375, ((0, 4), (1, 4))),
    }


rope_base = 1000000.0
norm_eps = 1e-06

def dequantize(tiles, scales, block):
    rows, cols = tiles.shape
    grid = tiles.reshape(rows // block, block, cols // block, block).astype(jnp.float32)
    scaled = grid * scales.astype(jnp.float32)[:, None, :, None]
    return scaled.reshape(rows, cols).astype(jnp.bfloat16)

def rotate(values, positions):
    half = values.shape[-1] // 2
    freq = rope_base ** (-jnp.arange(half, dtype=jnp.float32) / half)
    angle = positions.astype(jnp.float32)[:, None] * freq[None, :]
    cosine = jnp.cos(angle)[:, None, :]
    sine = jnp.sin(angle)[:, None, :]
    first = values[..., :half]
    second = values[..., half:]
    return jnp.concatenate([first * cosine - second * sine, second * cosine + first * sine], -1)

def reference(hidden_in, lengths, norm_gain, q_tiles, q_scales, kv_tiles, kv_scales, out_weight):
    group = QHEADS // KVHEADS
    positions = jnp.tile(jnp.arange(ROWS, dtype=jnp.int32), N_REPLICA)
    index = jnp.arange(ROWS, dtype=jnp.int32)
    causal = index[None, :] <= index[:, None]
    valid = causal[None, :, :] & (index[None, None, :] < lengths[:, None, None])
    hidden = hidden_in
    outputs = []
    caches = []
    for layer in range(LAYERS):
        w_query = dequantize(q_tiles[layer], q_scales[layer], BLOCK)
        w_keyval = dequantize(kv_tiles[layer], kv_scales[layer], BLOCK)
        values = hidden.astype(jnp.float32)
        scale = lax.rsqrt(lax.optimization_barrier(jnp.mean(values * values, -1, keepdims=True)) + norm_eps)
        normed = (values * scale * norm_gain[layer]).astype(jnp.bfloat16)
        query = jnp.dot(normed, w_query, preferred_element_type=jnp.float32).reshape(TOTAL_ROWS, QHEADS, HEAD)
        query = rotate(query, positions).astype(jnp.bfloat16)
        keyval = jnp.dot(normed, w_keyval, preferred_element_type=jnp.float32).reshape(TOTAL_ROWS, KVHEADS, 2, HEAD)
        keys = rotate(keyval[:, :, 0], positions).astype(jnp.bfloat16)
        vals = keyval[:, :, 1].astype(jnp.bfloat16)
        caches.append(jnp.stack([keys, vals], 2).reshape(TOTAL_ROWS, KVHEADS * 2 * HEAD))
        qr = query.reshape(N_REPLICA, ROWS, KVHEADS, group, HEAD).astype(jnp.float32)
        kr = keys.reshape(N_REPLICA, ROWS, KVHEADS, HEAD).astype(jnp.float32)
        vr = vals.reshape(N_REPLICA, ROWS, KVHEADS, HEAD).astype(jnp.float32)
        scores = jnp.einsum('rikgd,rjkd->rkgij', qr, kr) / jnp.sqrt(jnp.float32(HEAD))
        mask = valid[:, None, None, :, :]
        scores = jnp.where(mask, scores, -jnp.inf)
        top = lax.optimization_barrier(jnp.max(scores, -1, keepdims=True))
        expo = jnp.where(mask, jnp.exp(scores - top), 0.0)
        probs = (expo / lax.optimization_barrier(jnp.sum(expo, -1, keepdims=True))).astype(jnp.bfloat16)
        attended = jnp.einsum('rkgij,rjkd->rikgd', probs.astype(jnp.float32), vr)
        attended = attended.astype(jnp.bfloat16).reshape(TOTAL_ROWS, QHEADS * HEAD)
        width = QHEADS * HEAD // N_TENSOR
        total = jnp.zeros((TOTAL_ROWS, D), jnp.float32)
        for member in range(N_TENSOR):
            part = jnp.dot(attended[:, member * width:(member + 1) * width], out_weight[layer, member * width:(member + 1) * width], preferred_element_type=jnp.float32)
            total = total + part.astype(jnp.bfloat16).astype(jnp.float32)
        hidden = (hidden.astype(jnp.float32) + total).astype(jnp.bfloat16)
        outputs.append(hidden)
    return (jnp.stack(outputs, 0), jnp.stack(caches, 0))
```

```python
import functools

import jax
import jax.numpy as jnp
from jax import lax
from jax.experimental import pallas as pl
from jax.experimental.pallas import tpu as pltpu
from jax.sharding import PartitionSpec as P

HEAD = 128
BLOCK = 128
N_TILE = 256
OUT_TILE = 512
STRIP = 16

rope_base = 1000000.0
norm_eps = 1e-06

AXES = ("replica", "section", "tensor")
VMEM_LIMIT = 48 * 1024 * 1024


def project_kernel(pieces, replicas, q_steps, kv_steps, place, *refs):
    blocks = refs[:pieces]
    gain, q_tile, kv_tile, scale, out, held, square, weight = refs[pieces:]
    rows, width = blocks[0].shape
    step = pl.program_id(0)
    columns = pl.ds(pl.multiple_of(step * N_TILE, N_TILE), N_TILE)

    @pl.when(step == 0)
    def _():
        square[...] = jnp.zeros_like(square)
        for index, block in enumerate(blocks):
            slot = lax.rem(place[0] + pieces - index, pieces)
            top = lax.rem(slot, replicas) * rows
            left = lax.div(slot, replicas) * width
            span = pl.ds(pl.multiple_of(left, HEAD), width)

            def strip(number, _):
                source = pl.ds(pl.multiple_of(number * STRIP, STRIP), STRIP)
                target = pl.ds(pl.multiple_of(top + number * STRIP, STRIP), STRIP)
                values = block[source, :].astype(jnp.float32)
                held[target, span] = (values * gain[:, span]).astype(jnp.bfloat16)
                square[target, :] += jnp.sum(values * values, -1, keepdims=True)
                return 0

            lax.fori_loop(0, rows // STRIP, strip, 0)
        for replica in range(replicas):
            total = square[replica * rows:(replica + 1) * rows, :]
            coarse = total.astype(jnp.bfloat16)
            rest = (total - coarse.astype(jnp.float32)).astype(jnp.bfloat16)
            lane = lax.broadcasted_iota(jnp.int32, total.shape, 1)
            pair = jnp.where(lane < HEAD // 2, coarse.astype(jnp.float32), rest.astype(jnp.float32))
            out[replica, :, pl.ds((q_steps + kv_steps) * N_TILE, HEAD)] = pair.astype(jnp.bfloat16)

    def rescale(tile):
        for number in range(tile.shape[0] // BLOCK):
            span = pl.ds(number * BLOCK, BLOCK)
            factor = jnp.broadcast_to(scale[pl.ds(number, 1), columns], (BLOCK, N_TILE))
            weight[span, :] = (tile[span, :].astype(jnp.float32) * factor).astype(jnp.bfloat16)

    pl.when(step < q_steps)(lambda: rescale(q_tile))
    pl.when(step >= q_steps)(lambda: rescale(kv_tile))
    for replica in range(replicas):
        share = held[replica * rows:(replica + 1) * rows, :]
        product = jnp.dot(share, weight[...], preferred_element_type=jnp.float32)
        out[replica, :, columns] = product.astype(jnp.bfloat16)


def project(pieces, place, gain, q_tiles, kv_tiles, scales, replicas):
    rows, width = pieces[0].shape
    depth, q_cols = q_tiles.shape
    kv_cols = kv_tiles.shape[1]
    q_steps, kv_steps = q_cols // N_TILE, kv_cols // N_TILE
    total = q_cols + kv_cols + HEAD
    whole = lambda *shape: pl.BlockSpec(shape, lambda j, place: (0,) * len(shape))
    return pl.pallas_call(
        functools.partial(project_kernel, len(pieces), replicas, q_steps, kv_steps),
        grid_spec=pltpu.PrefetchScalarGridSpec(
            num_scalar_prefetch=1,
            grid=(q_steps + kv_steps,),
            in_specs=[whole(rows, width)] * len(pieces)
            + [
                whole(1, depth),
                pl.BlockSpec((depth, N_TILE), lambda j, place: (0, jnp.minimum(j, q_steps - 1))),
                pl.BlockSpec((depth, N_TILE), lambda j, place: (0, jnp.maximum(j - q_steps, 0))),
                whole(*scales.shape),
            ],
            out_specs=whole(replicas, rows, total),
            scratch_shapes=[
                pltpu.VMEM((replicas * rows, depth), jnp.bfloat16),
                pltpu.VMEM((replicas * rows, HEAD), jnp.float32),
                pltpu.VMEM((depth, N_TILE), jnp.bfloat16),
            ],
        ),
        out_shape=jax.ShapeDtypeStruct((replicas, rows, total), jnp.bfloat16),
        compiler_params=pltpu.CompilerParams(vmem_limit_bytes=VMEM_LIMIT),
        name="project",
    )(place, *pieces, gain, q_tiles, kv_tiles, scales)


def attend_kernel(q_heads, kv_heads, features, length, parts, cosine, sine, out, cache):
    replicas, rows, _ = parts.shape
    group = q_heads // kv_heads

    def total(start):
        value = parts[0, :, start:start + HEAD].astype(jnp.float32)
        for other in range(1, replicas):
            value = value + parts[other, :, start:start + HEAD].astype(jnp.float32)
        return value

    pair = total((q_heads + 2 * kv_heads) * HEAD)
    square = pair[:, :1] + pair[:, HEAD // 2:HEAD // 2 + 1]
    factor = jnp.broadcast_to(lax.rsqrt(square / features + norm_eps), (rows, HEAD))

    def rotate(value):
        return value * cosine[...] + pltpu.roll(value, HEAD // 2, 1) * sine[...]

    row = lax.broadcasted_iota(jnp.int32, (rows, rows), 0)
    col = lax.broadcasted_iota(jnp.int32, (rows, rows), 1)
    mask = jnp.concatenate([(col <= row) & (col < length[0])] * group, 0)
    for kv_head in range(kv_heads):
        start = (q_heads + 2 * kv_head) * HEAD
        keys = rotate(total(start) * factor).astype(jnp.bfloat16)
        values = (total(start + HEAD) * factor).astype(jnp.bfloat16)
        cache[:, 2 * kv_head * HEAD:(2 * kv_head + 1) * HEAD] = keys
        cache[:, (2 * kv_head + 1) * HEAD:(2 * kv_head + 2) * HEAD] = values
        heads = range(kv_head * group, (kv_head + 1) * group)
        query = jnp.concatenate(
            [rotate(total(head * HEAD) * factor).astype(jnp.bfloat16) for head in heads], 0
        )
        scores = lax.dot_general(
            query, keys, (((1,), (1,)), ((), ())), preferred_element_type=jnp.float32
        )
        scores = jnp.where(mask, scores / jnp.sqrt(jnp.float32(HEAD)), -jnp.inf)
        expo = jnp.exp(scores - jnp.max(scores, -1, keepdims=True))
        probs = (expo / jnp.sum(expo, -1, keepdims=True)).astype(jnp.bfloat16)
        mixed = jnp.dot(probs, values, preferred_element_type=jnp.float32).astype(jnp.bfloat16)
        for number, head in enumerate(heads):
            out[:, head * HEAD:(head + 1) * HEAD] = mixed[number * rows:(number + 1) * rows, :]


def attend(parts, length, cosine, sine, q_cols, kv_cols, features):
    rows = parts.shape[1]
    vmem = pl.BlockSpec(memory_space=pltpu.VMEM)
    return pl.pallas_call(
        functools.partial(attend_kernel, q_cols // HEAD, kv_cols // (2 * HEAD), features),
        in_specs=[pl.BlockSpec(memory_space=pltpu.SMEM), vmem, vmem, vmem],
        out_specs=[vmem, vmem],
        out_shape=[
            jax.ShapeDtypeStruct((rows, q_cols), jnp.bfloat16),
            jax.ShapeDtypeStruct((rows, kv_cols), jnp.bfloat16),
        ],
        compiler_params=pltpu.CompilerParams(vmem_limit_bytes=VMEM_LIMIT),
        name="attend",
    )(length, parts, cosine, sine)


def spread_kernel(attended, weight, out):
    product = jnp.dot(attended[...], weight[...], preferred_element_type=jnp.float32)
    out[...] = product.astype(jnp.bfloat16)


def spread(attended, weight, shards):
    rows, depth = attended.shape
    width = weight.shape[1] // shards
    tile = min(OUT_TILE, width)
    per = width // tile
    return pl.pallas_call(
        spread_kernel,
        grid=(shards * per,),
        in_specs=[
            pl.BlockSpec((rows, depth), lambda j: (0, 0)),
            pl.BlockSpec((depth, tile), lambda j: (0, j)),
        ],
        out_specs=pl.BlockSpec((None, rows, tile), lambda j: (j // per, 0, j % per)),
        out_shape=jax.ShapeDtypeStruct((shards, rows, width), jnp.bfloat16),
        compiler_params=pltpu.CompilerParams(vmem_limit_bytes=VMEM_LIMIT),
        name="spread",
    )(attended, weight)


def per_device(sizes, hidden_in, lengths, norm_gain, q_tiles, q_scales, kv_tiles, kv_scales, out_weight):
    replicas, sections, shards = sizes
    section = lax.axis_index("section")
    rows, width = hidden_in.shape
    features = norm_gain.shape[1]
    q_tiles, kv_tiles, w_out = q_tiles[0], kv_tiles[0], out_weight[0]
    depth, q_cols = q_tiles.shape
    kv_cols = kv_tiles.shape[1]
    per_slice = shards // replicas
    place = lax.axis_index("tensor").astype(jnp.int32)[None]
    gain = lax.dynamic_slice_in_dim(norm_gain, lax.axis_index("replica") * depth, depth, 1)
    scales = jnp.repeat(jnp.concatenate([q_scales[0], kv_scales[0]], 1).astype(jnp.float32), BLOCK, 1)
    half = HEAD // 2
    freq = rope_base ** (-jnp.arange(half, dtype=jnp.float32) / half)
    angle = jnp.arange(rows, dtype=jnp.float32)[:, None] * freq[None, :]
    cosine = jnp.concatenate([jnp.cos(angle)] * 2, 1)
    sine = jnp.concatenate([-jnp.sin(angle), jnp.sin(angle)], 1)

    def device(replica, sect, shard):
        return (replica * sections + sect) * shards + shard

    def gather(value, source_of, target):
        pieces = []
        for turn in range(shards):
            pairs = []
            for replica in range(replicas):
                for shard in range(shards):
                    goal = ((shard % per_slice) * replicas + replica + turn) % shards
                    pairs.append(
                        (
                            device(replica, source_of(turn), shard),
                            device(shard // per_slice, target, goal),
                        )
                    )
            pieces.append(lax.ppermute(value, AXES, pairs))
        return pieces

    hidden = hidden_in
    layer_out = jnp.zeros((rows, width), jnp.bfloat16)
    cache_out = jnp.zeros((rows, kv_cols), jnp.bfloat16)
    for layer in range(sections):
        if layer == 0:
            pieces = gather(hidden, lambda turn: turn % sections, 0)
            residual = hidden
        else:
            pieces = gather(layer_out, lambda turn: layer - 1, layer)
            pairs = [
                (device(replica, layer - 1, shard), device(replica, layer, shard))
                for replica in range(replicas)
                for shard in range(shards)
            ]
            residual = lax.ppermute(layer_out, AXES, pairs)

        def work(pieces, residual, layer_out, cache_out):
            parts = project(pieces, place, gain, q_tiles, kv_tiles, scales, replicas)
            parts = lax.all_to_all(parts, "replica", 0, 0, tiled=True)
            attended, cache = attend(parts, lengths, cosine, sine, q_cols, kv_cols, features)
            partials = spread(attended, w_out, shards)
            partials = lax.all_to_all(partials, "tensor", 0, 0, tiled=True)
            total = residual.astype(jnp.float32) + jnp.sum(partials.astype(jnp.float32), 0)
            return total.astype(jnp.bfloat16), cache

        def rest(pieces, residual, layer_out, cache_out):
            return layer_out, cache_out

        layer_out, cache_out = lax.cond(
            section == layer, work, rest, pieces, residual, layer_out, cache_out
        )
    return layer_out[None], cache_out[None]


def solution(mesh):
    sizes = tuple(mesh.shape[axis] for axis in AXES)
    in_specs = (
        P("replica", "tensor"),
        P("replica"),
        P("section", None),
        P("section", "replica", "tensor"),
        P("section", "replica", "tensor"),
        P("section", "replica", "tensor"),
        P("section", "replica", "tensor"),
        P("section", "tensor", None),
    )
    out_specs = (P("section", "replica", "tensor"), P("section", "replica", "tensor"))
    return jax.shard_map(
        functools.partial(per_device, sizes),
        mesh=mesh,
        in_specs=in_specs,
        out_specs=out_specs,
        check_vma=False,
    )
```

```python
import functools

import jax
import jax.numpy as jnp
from jax import lax
from jax.experimental import pallas as pl
from jax.experimental.pallas import tpu as pltpu
from jax.sharding import PartitionSpec as P

HEAD = 128
BLOCK = 128
STRIP = 16
TILE = 512

rope_base = 1000000.0
norm_eps = 1e-06

AXES = ("replica", "section", "tensor")
PARAMS = pltpu.CompilerParams(vmem_limit_bytes=24 * 1024 * 1024)
IN_VMEM = pl.BlockSpec(memory_space=pltpu.VMEM)
IN_SMEM = pl.BlockSpec(memory_space=pltpu.SMEM)
IN_HBM = pl.BlockSpec(memory_space=pl.ANY)


def cost(flops, moved):
    return pl.CostEstimate(flops=flops, bytes_accessed=moved, transcendentals=0)


def resident(value):
    return pltpu.with_memory_space_constraint(value, pltpu.VMEM)


def tiles_of(columns):
    return [(start, min(TILE, columns - start)) for start in range(0, columns, TILE)]


def rescale_kernel(q_tile, kv_tile, scale, out):
    step = pl.program_id(0)
    q_cols = q_tile.shape[1]
    chunk = q_tile.shape[0]
    for number in range(chunk // BLOCK):
        source = pl.ds(number * BLOCK, BLOCK)
        target = pl.ds(pl.multiple_of(step * chunk + number * BLOCK, BLOCK), BLOCK)
        line = scale[pl.ds(step * (chunk // BLOCK) + number, 1), :]
        for tile, left in ((q_tile, 0), (kv_tile, q_cols)):
            width = tile.shape[1]
            factor = jnp.broadcast_to(line[:, left:left + width], (BLOCK, width))
            value = tile[source, :].astype(jnp.float32) * factor
            out[target, left:left + width] = value.astype(jnp.bfloat16)


def rescale(q_tiles, kv_tiles, scales):
    depth, q_cols = q_tiles.shape
    kv_cols = kv_tiles.shape[1]
    chunk = min(TILE, depth)
    return pl.pallas_call(
        rescale_kernel,
        grid=(depth // chunk,),
        in_specs=[
            pl.BlockSpec((chunk, q_cols), lambda i: (i, 0)),
            pl.BlockSpec((chunk, kv_cols), lambda i: (i, 0)),
            pl.BlockSpec(scales.shape, lambda i: (0, 0)),
        ],
        out_specs=IN_VMEM,
        out_shape=pltpu.VMEM((depth, q_cols + kv_cols), jnp.bfloat16),
        compiler_params=PARAMS,
        cost_estimate=cost(depth * (q_cols + kv_cols), 2 * depth * (q_cols + kv_cols)),
        name="rescale",
    )(q_tiles, kv_tiles, scales)


def fetch_kernel(source, target, done):
    parts = done.shape[0]
    rows = source.shape[0] // parts
    copies = []
    for part in range(parts):
        span = pl.ds(part * rows, rows)
        copies.append(pltpu.make_async_copy(source.at[span], target.at[span], done.at[part]))
    for copy in copies:
        copy.start()
    for copy in copies:
        copy.wait()


def fetch(weight):
    return pl.pallas_call(
        fetch_kernel,
        in_specs=[IN_HBM],
        out_specs=IN_VMEM,
        out_shape=pltpu.VMEM(weight.shape, weight.dtype),
        scratch_shapes=[pltpu.SemaphoreType.DMA((4,))],
        compiler_params=PARAMS,
        cost_estimate=cost(0, 2 * weight.size),
        name="fetch",
    )(weight)


def project_kernel(turn, pieces, replicas, place, piece, gain, weight, *refs):
    if turn == 0:
        before, after = None, refs[0]
    else:
        before, after = refs[0], refs[1]
    rows, width = piece.shape
    columns = weight.shape[1]
    slot = lax.rem(place[1] + pieces - turn, pieces)
    replica = lax.rem(slot, replicas)
    span = pl.ds(pl.multiple_of(lax.div(slot, replicas) * width, HEAD), width)
    held = refs[-1]
    squares = []
    for start in range(0, rows, STRIP):
        values = piece[start:start + STRIP, :].astype(jnp.float32)
        held[start:start + STRIP, :] = (values * gain[:, span]).astype(jnp.bfloat16)
        squares.append(jnp.sum(values * values, -1, keepdims=True))
    square = jnp.broadcast_to(jnp.concatenate(squares, 0), (rows, HEAD))
    if turn == 0:
        after[...] = jnp.zeros_like(after)
    tail = pl.ds(columns, HEAD)
    after[replica, :, tail] = square if turn == 0 else before[replica, :, tail] + square
    for start, size in tiles_of(columns):
        part = pl.ds(start, size)
        product = jnp.dot(held[...], weight[span, part], preferred_element_type=jnp.float32)
        after[replica, :, part] = product if turn == 0 else before[replica, :, part] + product
    if turn == pieces - 1:
        own, sends = refs[2], refs[3:-1]
        own[...] = after[place[0]]
        for other, send in enumerate(sends, 1):
            goal = lax.rem(place[0] + other, replicas)
            send[:, :columns] = after[goal, :, pl.ds(0, columns)].astype(jnp.bfloat16)
            total = after[goal, :, tail]
            coarse = total.astype(jnp.bfloat16).astype(jnp.float32)
            lane = lax.broadcasted_iota(jnp.int32, total.shape, 1)
            pair = jnp.where(lane < HEAD // 2, coarse, total - coarse)
            send[:, columns:] = pair.astype(jnp.bfloat16)


def project(turn, pieces, replicas, place, piece, gain, weight, total):
    rows, width = piece.shape
    columns = weight.shape[1] + HEAD
    out_shape = [jax.ShapeDtypeStruct((replicas, rows, columns), jnp.float32)]
    if turn == pieces - 1:
        out_shape.append(jax.ShapeDtypeStruct((rows, columns), jnp.float32))
        out_shape += [jax.ShapeDtypeStruct((rows, columns), jnp.bfloat16)] * (replicas - 1)
    before = [] if turn == 0 else [total]
    return pl.pallas_call(
        functools.partial(project_kernel, turn, pieces, replicas),
        in_specs=[IN_SMEM] + [IN_VMEM] * (3 + len(before)),
        out_specs=[IN_VMEM] * len(out_shape),
        out_shape=out_shape,
        scratch_shapes=[pltpu.VMEM((rows, width), jnp.bfloat16)],
        input_output_aliases={4: 0} if before else {},
        compiler_params=PARAMS,
        cost_estimate=cost(8 * rows * width * columns, 2 * width * columns),
        name="project",
    )(place, piece, gain, resident(weight), *before)


def attend_kernel(q_heads, kv_heads, features, length, own, *refs):
    received = refs[:-4]
    cosine, sine, out, cache = refs[-4:]
    rows = own.shape[0]
    group = q_heads // kv_heads

    def total(start):
        value = own[:, start:start + HEAD]
        for part in received:
            value = value + part[:, start:start + HEAD].astype(jnp.float32)
        return value

    tail = (q_heads + 2 * kv_heads) * HEAD
    square = own[:, tail:tail + 1]
    for part in received:
        pair = part[:, tail:].astype(jnp.float32)
        square = square + (pair[:, :1] + pair[:, HEAD // 2:HEAD // 2 + 1])
    factor = jnp.broadcast_to(lax.rsqrt(square / features + norm_eps), (rows, HEAD))

    def rotate(value):
        return value * cosine[...] + pltpu.roll(value, HEAD // 2, 1) * sine[...]

    row = lax.broadcasted_iota(jnp.int32, (rows, rows), 0)
    col = lax.broadcasted_iota(jnp.int32, (rows, rows), 1)
    mask = jnp.concatenate([(col <= row) & (col < length[0])] * group, 0)
    for kv_head in range(kv_heads):
        start = (q_heads + 2 * kv_head) * HEAD
        keys = rotate(total(start) * factor).astype(jnp.bfloat16)
        values = (total(start + HEAD) * factor).astype(jnp.bfloat16)
        cache[:, 2 * kv_head * HEAD:(2 * kv_head + 1) * HEAD] = keys
        cache[:, (2 * kv_head + 1) * HEAD:(2 * kv_head + 2) * HEAD] = values
        heads = range(kv_head * group, (kv_head + 1) * group)
        query = jnp.concatenate(
            [rotate(total(head * HEAD) * factor).astype(jnp.bfloat16) for head in heads], 0
        )
        scores = lax.dot_general(
            query, keys, (((1,), (1,)), ((), ())), preferred_element_type=jnp.float32
        )
        scores = jnp.where(mask, scores / jnp.sqrt(jnp.float32(HEAD)), -jnp.inf)
        expo = jnp.exp(scores - jnp.max(scores, -1, keepdims=True))
        probs = (expo / jnp.sum(expo, -1, keepdims=True)).astype(jnp.bfloat16)
        mixed = jnp.dot(probs, values, preferred_element_type=jnp.float32).astype(jnp.bfloat16)
        for number, head in enumerate(heads):
            out[:, head * HEAD:(head + 1) * HEAD] = mixed[number * rows:(number + 1) * rows, :]


def attend(own, received, length, cosine, sine, q_cols, kv_cols, features):
    rows = own.shape[0]
    return pl.pallas_call(
        functools.partial(attend_kernel, q_cols // HEAD, kv_cols // (2 * HEAD), features),
        in_specs=[IN_SMEM] + [IN_VMEM] * (3 + len(received)),
        out_specs=[IN_VMEM, IN_VMEM],
        out_shape=[
            jax.ShapeDtypeStruct((rows, q_cols), jnp.bfloat16),
            jax.ShapeDtypeStruct((rows, kv_cols), jnp.bfloat16),
        ],
        compiler_params=PARAMS,
        cost_estimate=cost(16 * rows * rows * q_cols, 6 * rows * (q_cols + kv_cols)),
        name="attend",
    )(length, own, *received, cosine, sine)


def spread_kernel(turn, shards, place, attended, weight, out):
    width = out.shape[1]
    goal = lax.rem(place[1] + turn, shards)
    for start, size in tiles_of(width):
        span = pl.ds(pl.multiple_of(goal * width + start, HEAD), size)
        product = jnp.dot(attended[...], weight[:, span], preferred_element_type=jnp.float32)
        out[:, start:start + size] = product.astype(jnp.bfloat16)


def spread(turn, shards, place, attended, weight):
    rows, depth = attended.shape
    width = weight.shape[1] // shards
    return pl.pallas_call(
        functools.partial(spread_kernel, turn, shards),
        in_specs=[IN_SMEM, IN_VMEM, IN_VMEM],
        out_specs=IN_VMEM,
        out_shape=jax.ShapeDtypeStruct((rows, width), jnp.bfloat16),
        compiler_params=PARAMS,
        cost_estimate=cost(8 * rows * width * depth, 2 * depth * width),
        name="spread",
    )(place, attended, resident(weight))


def per_device(sizes, hidden_in, lengths, norm_gain, q_tiles, q_scales, kv_tiles, kv_scales, out_weight):
    replicas, sections, shards = sizes
    section = lax.axis_index("section")
    rows, width = hidden_in.shape
    features = norm_gain.shape[1]
    q_tiles, kv_tiles = q_tiles[0], kv_tiles[0]
    depth, q_cols = q_tiles.shape
    kv_cols = kv_tiles.shape[1]
    per_slice = shards // replicas
    place = jnp.stack([lax.axis_index("replica"), lax.axis_index("tensor")]).astype(jnp.int32)
    gain = lax.dynamic_slice_in_dim(norm_gain, lax.axis_index("replica") * depth, depth, 1)
    scales = jnp.repeat(jnp.concatenate([q_scales[0], kv_scales[0]], 1).astype(jnp.float32), BLOCK, 1)
    half = HEAD // 2
    freq = rope_base ** (-jnp.arange(half, dtype=jnp.float32) / half)
    angle = jnp.arange(rows, dtype=jnp.float32)[:, None] * freq[None, :]
    cosine = jnp.concatenate([jnp.cos(angle)] * 2, 1)
    sine = jnp.concatenate([-jnp.sin(angle), jnp.sin(angle)], 1)
    w_in = rescale(q_tiles, kv_tiles, scales)
    w_out = fetch(out_weight[0])

    def device(replica, sect, shard):
        return (replica * sections + sect) * shards + shard

    def move(value, pair_of):
        pairs = []
        for replica in range(replicas):
            for shard in range(shards):
                source, target = pair_of(replica, shard)
                pairs.append((device(*source), device(*target)))
        return lax.ppermute(value, AXES, pairs)

    def gather(value, source_of, target):
        def pair_of(turn, replica, shard):
            goal = ((shard % per_slice) * replicas + replica + turn) % shards
            return (replica, source_of(turn), shard), (shard // per_slice, target, goal)

        return [move(value, functools.partial(pair_of, turn)) for turn in range(shards)]

    turns = sorted(range(1, shards), key=lambda turn: -min(turn, shards - turn))
    layer_out, cache_out = hidden_in, None
    for layer in range(sections):
        if layer == 0:
            pieces = gather(hidden_in, lambda turn: turn % sections, 0)
            residual = hidden_in
        else:
            pieces = gather(result, lambda turn: layer - 1, layer)
            residual = move(
                result, lambda replica, shard: ((replica, layer - 1, shard), (replica, layer, shard))
            )
        total = None
        for turn, piece in enumerate(pieces):
            outs = project(turn, shards, replicas, place, piece, gain, w_in, total)
            total = outs[0]
        own, sends = outs[1], outs[2:]
        received = [
            move(
                send,
                lambda replica, shard: (
                    (replica, layer, shard),
                    ((replica + other) % replicas, layer, shard),
                ),
            )
            for other, send in enumerate(sends, 1)
        ]
        attended, cache = attend(own, received, lengths, cosine, sine, q_cols, kv_cols, features)
        arrived = []
        for turn in turns:
            partial = spread(turn, shards, place, attended, w_out)
            arrived.append(
                move(
                    partial,
                    lambda replica, shard: (
                        (replica, layer, shard),
                        (replica, layer, (shard + turn) % shards),
                    ),
                )
            )
        summed = spread(0, shards, place, attended, w_out).astype(jnp.float32)
        for partial in arrived:
            summed = summed + partial.astype(jnp.float32)
        result = (residual.astype(jnp.float32) + summed).astype(jnp.bfloat16)
        if layer == 0:
            layer_out, cache_out = result, cache
        else:
            layer_out = jnp.where(section == layer, result, layer_out)
            cache_out = jnp.where(section == layer, cache, cache_out)
    return layer_out[None], cache_out[None]


def solution(mesh):
    sizes = tuple(mesh.shape[axis] for axis in AXES)
    in_specs = (
        P("replica", "tensor"),
        P("replica"),
        P("section", None),
        P("section", "replica", "tensor"),
        P("section", "replica", "tensor"),
        P("section", "replica", "tensor"),
        P("section", "replica", "tensor"),
        P("section", "tensor", None),
    )
    out_specs = (P("section", "replica", "tensor"), P("section", "replica", "tensor"))
    return jax.shard_map(
        functools.partial(per_device, sizes),
        mesh=mesh,
        in_specs=in_specs,
        out_specs=out_specs,
        check_vma=False,
    )
```

```python
import functools

import jax
import jax.numpy as jnp
from jax import lax
from jax.experimental import pallas as pl
from jax.experimental.pallas import tpu as pltpu
from jax.sharding import PartitionSpec as P

HEAD = 128
BLOCK = 128
STRIP = 16
TILE = 512

rope_base = 1000000.0
norm_eps = 1e-06

AXES = ("replica", "section", "tensor")
PARAMS = pltpu.CompilerParams(vmem_limit_bytes=8 * 1024 * 1024)
IN_VMEM = pl.BlockSpec(memory_space=pltpu.VMEM)
IN_SMEM = pl.BlockSpec(memory_space=pltpu.SMEM)
IN_HBM = pl.BlockSpec(memory_space=pl.ANY)


def cost(flops, moved):
    return pl.CostEstimate(flops=flops, bytes_accessed=moved, transcendentals=0)


def resident(value):
    return pltpu.with_memory_space_constraint(value, pltpu.VMEM)


def tiles_of(columns):
    return [(start, min(TILE, columns - start)) for start in range(0, columns, TILE)]


def rescale_kernel(q_tile, kv_tile, scale, out):
    step = pl.program_id(0)
    q_cols = q_tile.shape[1]
    chunk = q_tile.shape[0]
    for number in range(chunk // BLOCK):
        source = pl.ds(number * BLOCK, BLOCK)
        target = pl.ds(pl.multiple_of(step * chunk + number * BLOCK, BLOCK), BLOCK)
        line = scale[pl.ds(step * (chunk // BLOCK) + number, 1), :]
        for tile, left in ((q_tile, 0), (kv_tile, q_cols)):
            width = tile.shape[1]
            factor = jnp.broadcast_to(line[:, left:left + width], (BLOCK, width))
            value = tile[source, :].astype(jnp.float32) * factor
            out[target, left:left + width] = value.astype(jnp.bfloat16)


def rescale(q_tiles, kv_tiles, scales):
    depth, q_cols = q_tiles.shape
    kv_cols = kv_tiles.shape[1]
    chunk = min(TILE, depth)
    return pl.pallas_call(
        rescale_kernel,
        grid=(depth // chunk,),
        in_specs=[
            pl.BlockSpec((chunk, q_cols), lambda i: (i, 0)),
            pl.BlockSpec((chunk, kv_cols), lambda i: (i, 0)),
            pl.BlockSpec(scales.shape, lambda i: (0, 0)),
        ],
        out_specs=IN_VMEM,
        out_shape=pltpu.VMEM((depth, q_cols + kv_cols), jnp.bfloat16),
        compiler_params=PARAMS,
        cost_estimate=cost(depth * (q_cols + kv_cols), 2 * depth * (q_cols + kv_cols)),
        name="rescale",
    )(q_tiles, kv_tiles, scales)


def fetch_kernel(source, target, done):
    parts = done.shape[0]
    rows = source.shape[0] // parts
    copies = []
    for part in range(parts):
        span = pl.ds(part * rows, rows)
        copies.append(pltpu.make_async_copy(source.at[span], target.at[span], done.at[part]))
    for copy in copies:
        copy.start()
    for copy in copies:
        copy.wait()


def fetch(weight):
    return pl.pallas_call(
        fetch_kernel,
        in_specs=[IN_HBM],
        out_specs=IN_VMEM,
        out_shape=pltpu.VMEM(weight.shape, weight.dtype),
        scratch_shapes=[pltpu.SemaphoreType.DMA((4,))],
        compiler_params=PARAMS,
        cost_estimate=cost(0, 2 * weight.size),
        name="fetch",
    )(weight)


def project_kernel(turns, pieces, natural, replicas, behind, last, place, *refs):
    count = len(turns)
    blocks, gain, weight = refs[:count], refs[count], refs[count + 1]
    rows, width = blocks[0].shape
    columns = weight.shape[1]
    total, held, result = refs[-2], refs[-1], refs[-3]
    if len(refs) == count + 6:
        total[...] = refs[count + 2][...]
    else:
        total[...] = jnp.zeros_like(total)
    wanted = lax.rem(place[0] + replicas - behind, replicas)

    def add(block, number):
        span = pl.ds(pl.multiple_of(number * width, HEAD), width)
        squares = []
        for start in range(0, rows, STRIP):
            values = block[start:start + STRIP, :].astype(jnp.float32)
            held[start:start + STRIP, :] = (values * gain[:, span]).astype(jnp.bfloat16)
            squares.append(jnp.sum(values * values, -1, keepdims=True))
        square = jnp.broadcast_to(jnp.concatenate(squares, 0), (rows, HEAD))
        total[:, columns:] += square
        for start, size in tiles_of(columns):
            product = jnp.dot(
                held[...], weight[span, start:start + size], preferred_element_type=jnp.float32
            )
            total[:, start:start + size] += product

    for turn, block in zip(turns, blocks):
        number = lax.rem(place[1] + pieces - turn, pieces)
        if natural:
            part = lax.div(number, replicas)
            pl.when(lax.rem(number, replicas) == wanted)(functools.partial(add, block, part))
        else:
            add(block, number)
    if last and behind:
        result[:, :columns] = total[:, :columns].astype(jnp.bfloat16)
        square = total[:, columns:]
        coarse = square.astype(jnp.bfloat16).astype(jnp.float32)
        lane = lax.broadcasted_iota(jnp.int32, square.shape, 1)
        result[:, columns:] = jnp.where(lane < HEAD // 2, coarse, square - coarse).astype(jnp.bfloat16)
    else:
        result[...] = total[...]


def project(turns, blocks, pieces, natural, replicas, behind, last, place, gain, weight, before):
    rows, width = blocks[0].shape
    columns = weight.shape[1] + HEAD
    kind = jnp.bfloat16 if last and behind else jnp.float32
    earlier = [] if before is None else [before]
    return pl.pallas_call(
        functools.partial(project_kernel, turns, pieces, natural, replicas, behind, last),
        in_specs=[IN_SMEM] + [IN_VMEM] * (len(blocks) + 2 + len(earlier)),
        out_specs=IN_VMEM,
        out_shape=jax.ShapeDtypeStruct((rows, columns), kind),
        scratch_shapes=[
            pltpu.VMEM((rows, columns), jnp.float32),
            pltpu.VMEM((rows, width), jnp.bfloat16),
        ],
        compiler_params=PARAMS,
        cost_estimate=cost(6 * len(blocks) * rows * width * columns, 2 * len(blocks) * width * columns),
        name="project",
    )(place, *blocks, gain, resident(weight), *earlier)


def attend_kernel(q_heads, kv_heads, features, length, own, *refs):
    received = refs[:-4]
    cosine, sine, out, cache = refs[-4:]
    rows = own.shape[0]
    group = q_heads // kv_heads

    def total(start):
        value = own[:, start:start + HEAD]
        for part in received:
            value = value + part[:, start:start + HEAD].astype(jnp.float32)
        return value

    tail = (q_heads + 2 * kv_heads) * HEAD
    square = own[:, tail:tail + 1]
    for part in received:
        pair = part[:, tail:].astype(jnp.float32)
        square = square + (pair[:, :1] + pair[:, HEAD // 2:HEAD // 2 + 1])
    factor = jnp.broadcast_to(lax.rsqrt(square / features + norm_eps), (rows, HEAD))

    def rotate(value):
        return value * cosine[...] + pltpu.roll(value, HEAD // 2, 1) * sine[...]

    row = lax.broadcasted_iota(jnp.int32, (rows, rows), 0)
    col = lax.broadcasted_iota(jnp.int32, (rows, rows), 1)
    mask = jnp.concatenate([(col <= row) & (col < length[0])] * group, 0)
    for kv_head in range(kv_heads):
        start = (q_heads + 2 * kv_head) * HEAD
        keys = rotate(total(start) * factor).astype(jnp.bfloat16)
        values = (total(start + HEAD) * factor).astype(jnp.bfloat16)
        cache[:, 2 * kv_head * HEAD:(2 * kv_head + 1) * HEAD] = keys
        cache[:, (2 * kv_head + 1) * HEAD:(2 * kv_head + 2) * HEAD] = values
        heads = range(kv_head * group, (kv_head + 1) * group)
        query = jnp.concatenate(
            [rotate(total(head * HEAD) * factor).astype(jnp.bfloat16) for head in heads], 0
        )
        scores = lax.dot_general(
            query, keys, (((1,), (1,)), ((), ())), preferred_element_type=jnp.float32
        )
        scores = jnp.where(mask, scores / jnp.sqrt(jnp.float32(HEAD)), -jnp.inf)
        expo = jnp.exp(scores - jnp.max(scores, -1, keepdims=True))
        probs = (expo / jnp.sum(expo, -1, keepdims=True)).astype(jnp.bfloat16)
        mixed = jnp.dot(probs, values, preferred_element_type=jnp.float32).astype(jnp.bfloat16)
        for number, head in enumerate(heads):
            out[:, head * HEAD:(head + 1) * HEAD] = mixed[number * rows:(number + 1) * rows, :]


def attend(own, received, length, cosine, sine, q_cols, kv_cols, features):
    rows = own.shape[0]
    return pl.pallas_call(
        functools.partial(attend_kernel, q_cols // HEAD, kv_cols // (2 * HEAD), features),
        in_specs=[IN_SMEM] + [IN_VMEM] * (3 + len(received)),
        out_specs=[IN_VMEM, IN_VMEM],
        out_shape=[
            jax.ShapeDtypeStruct((rows, q_cols), jnp.bfloat16),
            jax.ShapeDtypeStruct((rows, kv_cols), jnp.bfloat16),
        ],
        compiler_params=PARAMS,
        cost_estimate=cost(16 * rows * rows * q_cols, 6 * rows * (q_cols + kv_cols)),
        name="attend",
    )(length, own, *received, cosine, sine)


def spread_kernel(turn, shards, place, attended, weight, out):
    parts, _, width = out.shape
    goal = lax.rem(place[1] + turn, shards)
    for part in range(parts):
        if parts == 1:
            left = goal * width
        else:
            left = (lax.rem(place[0] + part, parts) * shards + goal) * width
        for start, size in tiles_of(width):
            span = pl.ds(pl.multiple_of(left + start, HEAD), size)
            product = jnp.dot(attended[...], weight[:, span], preferred_element_type=jnp.float32)
            out[part, :, start:start + size] = product.astype(jnp.bfloat16)


def spread(turn, shards, parts, place, attended, weight):
    rows, depth = attended.shape
    width = weight.shape[1] // (shards * parts)
    return pl.pallas_call(
        functools.partial(spread_kernel, turn, shards),
        in_specs=[IN_SMEM, IN_VMEM, IN_VMEM],
        out_specs=IN_VMEM,
        out_shape=jax.ShapeDtypeStruct((parts, rows, width), jnp.bfloat16),
        compiler_params=PARAMS,
        cost_estimate=cost(6 * rows * width * parts * depth, 2 * depth * width * parts),
        name="spread",
    )(place, attended, resident(weight))


def per_device(sizes, hidden_in, lengths, norm_gain, q_tiles, q_scales, kv_tiles, kv_scales, out_weight):
    replicas, sections, shards = sizes
    section = lax.axis_index("section")
    me, lane = lax.axis_index("replica"), lax.axis_index("tensor")
    rows, width = hidden_in.shape
    features = norm_gain.shape[1]
    q_tiles, kv_tiles = q_tiles[0], kv_tiles[0]
    depth, q_cols = q_tiles.shape
    kv_cols = kv_tiles.shape[1]
    per_slice = shards // replicas
    cell = width // replicas
    place = jnp.stack([me, lane]).astype(jnp.int32)
    gain = lax.dynamic_slice_in_dim(norm_gain, me * depth, depth, 1)
    scales = jnp.repeat(jnp.concatenate([q_scales[0], kv_scales[0]], 1).astype(jnp.float32), BLOCK, 1)
    half = HEAD // 2
    freq = rope_base ** (-jnp.arange(half, dtype=jnp.float32) / half)
    angle = jnp.arange(rows, dtype=jnp.float32)[:, None] * freq[None, :]
    cosine = jnp.concatenate([jnp.cos(angle)] * 2, 1)
    sine = jnp.concatenate([-jnp.sin(angle), jnp.sin(angle)], 1)
    w_in = rescale(q_tiles, kv_tiles, scales)
    w_out = fetch(lax.optimization_barrier((out_weight, w_in))[0][0])

    def device(replica, sect, shard):
        return (replica * sections + sect) * shards + shard

    def move(value, pair_of):
        pairs = []
        for replica in range(replicas):
            for shard in range(shards):
                source, target = pair_of(replica, shard)
                pairs.append((device(*source), device(*target)))
        return lax.ppermute(value, AXES, pairs)

    def pick(values, index):
        return lax.dynamic_index_in_dim(jnp.stack(values), index, 0, keepdims=False)

    def interleave(value, origin, target):
        came = []
        for turn in range(replicas):
            start = lax.rem(lane // per_slice + turn, replicas) * cell
            came.append(
                move(
                    lax.dynamic_slice_in_dim(value, start, cell, 1),
                    lambda replica, shard: (
                        (replica, origin, shard),
                        (
                            replica,
                            target,
                            shard % per_slice * replicas + (shard // per_slice + turn) % replicas,
                        ),
                    ),
                )
            )
        return [pick(came, jnp.mod(lane - me - part, replicas)) for part in range(replicas)]

    def restore(cells, layer):
        came = []
        for turn in range(replicas):
            came.append(
                move(
                    pick(cells, jnp.mod(lane + turn - me, replicas)),
                    lambda replica, shard: (
                        (replica, layer, shard),
                        (replica, layer, (shard + turn) % replicas * per_slice + shard // replicas),
                    ),
                )
            )
        slots = [pick(came, jnp.mod(lane // per_slice - slot, replicas)) for slot in range(replicas)]
        return jnp.concatenate(slots, 1)

    def gather_natural(value):
        def pair_of(turn, replica, shard):
            goal = (shard % per_slice * replicas + replica + turn) % shards
            return (replica, turn % sections, shard), (shard // per_slice, 0, goal)

        return [move(value, functools.partial(pair_of, turn)) for turn in range(shards)]

    def gather_cells(value, part, layer):
        def pair_of(turn, replica, shard):
            goal = ((replica + part) % replicas, layer + 1, (shard + turn) % shards)
            return (replica, layer, shard), goal

        return [move(value, functools.partial(pair_of, turn)) for turn in far_first]

    far_first = sorted(range(shards), key=lambda turn: -min(turn, shards - turn))
    order = list(range(1, replicas)) + [0]
    layer_out, cache_out = None, None
    residual = interleave(hidden_in, sections - 1, 0)
    pieces = gather_natural(hidden_in)
    for layer in range(sections):
        final = layer == sections - 1
        received = []
        for behind in order:
            turns = list(range(shards)) if layer == 0 else far_first
            blocks = pieces if layer == 0 else pieces[behind]
            if received:
                blocks = lax.optimization_barrier((blocks, ready))[0]
            total = None
            if layer == 0:
                groups = [range(shards)]
            else:
                groups = [range(shards // 2), range(shards // 2, shards)]
            for group in groups:
                total = project(
                    [turns[i] for i in group],
                    [blocks[i] for i in group],
                    shards,
                    layer == 0,
                    replicas,
                    behind,
                    group is groups[-1],
                    place,
                    gain,
                    w_in,
                    total,
                )
            if behind:
                ready = total
                received.append(
                    move(
                        total,
                        lambda replica, shard: (
                            (replica, layer, shard),
                            ((replica - behind) % replicas, layer, shard),
                        ),
                    )
                )
        attended, cache = attend(total, received, lengths, cosine, sine, q_cols, kv_cols, features)
        parts = 1 if final else replicas
        arrived = []
        for turn in far_first:
            partial = spread(turn, shards, parts, place, attended, w_out)
            if turn:
                partial = move(
                    partial,
                    lambda replica, shard: (
                        (replica, layer, shard),
                        (replica, layer, (shard + turn) % shards),
                    ),
                )
            arrived.append(partial)
        result = []
        for part in range(parts):
            value = residual[part].astype(jnp.float32)
            for partial in arrived:
                value = value + partial[part].astype(jnp.float32)
            result.append(value.astype(jnp.bfloat16))
        if final:
            natural = result[0]
        else:
            pieces = {}
            for part in order:
                pieces[part] = gather_cells(result[part], part, layer)
            natural = restore(result, layer)
            along = lambda replica, shard: ((replica, layer, shard), (replica, layer + 1, shard))
            if layer == sections - 2:
                residual = [move(natural, along)]
            else:
                residual = [move(value, along) for value in result]
        if layer == 0:
            layer_out, cache_out = natural, cache
        else:
            layer_out = jnp.where(section == layer, natural, layer_out)
            cache_out = jnp.where(section == layer, cache, cache_out)
        if not final:
            layer_out, cache_out = lax.optimization_barrier((layer_out, cache_out))
    return layer_out[None], cache_out[None]


def solution(mesh):
    sizes = tuple(mesh.shape[axis] for axis in AXES)
    in_specs = (
        P("replica", "tensor"),
        P("replica"),
        P("section", None),
        P("section", "replica", "tensor"),
        P("section", "replica", "tensor"),
        P("section", "replica", "tensor"),
        P("section", "replica", "tensor"),
        P("section", "tensor", None),
    )
    out_specs = (P("section", "replica", "tensor"), P("section", "replica", "tensor"))
    return jax.shard_map(
        functools.partial(per_device, sizes),
        mesh=mesh,
        in_specs=in_specs,
        out_specs=out_specs,
        check_vma=False,
    )
```

```python
import functools

import jax
import jax.numpy as jnp
from jax import lax
from jax.experimental import pallas as pl
from jax.experimental.pallas import tpu as pltpu
from jax.sharding import PartitionSpec as P

HEAD = 128
BLOCK = 128
STRIP = 16
TILE = 512

rope_base = 1000000.0
norm_eps = 1e-06

AXES = ("replica", "section", "tensor")
PARAMS = pltpu.CompilerParams(vmem_limit_bytes=8 * 1024 * 1024)
IN_VMEM = pl.BlockSpec(memory_space=pltpu.VMEM)
IN_SMEM = pl.BlockSpec(memory_space=pltpu.SMEM)
IN_HBM = pl.BlockSpec(memory_space=pl.ANY)


def cost(flops, moved):
    return pl.CostEstimate(flops=flops, bytes_accessed=moved, transcendentals=0)


def resident(value):
    return pltpu.with_memory_space_constraint(value, pltpu.VMEM)


def in_hbm(value):
    return pltpu.with_memory_space_constraint(value, pltpu.HBM)


def tiles_of(columns):
    return [(start, min(TILE, columns - start)) for start in range(0, columns, TILE)]


def rescale_kernel(q_tile, kv_tile, scale, out):
    step = pl.program_id(0)
    q_cols = q_tile.shape[1]
    chunk = q_tile.shape[0]
    for number in range(chunk // BLOCK):
        source = pl.ds(number * BLOCK, BLOCK)
        target = pl.ds(pl.multiple_of(step * chunk + number * BLOCK, BLOCK), BLOCK)
        line = scale[pl.ds(step * (chunk // BLOCK) + number, 1), :]
        for tile, left in ((q_tile, 0), (kv_tile, q_cols)):
            width = tile.shape[1]
            factor = jnp.broadcast_to(line[:, left:left + width], (BLOCK, width))
            value = tile[source, :].astype(jnp.float32) * factor
            out[target, left:left + width] = value.astype(jnp.bfloat16)


def rescale(q_tiles, kv_tiles, scales):
    depth, q_cols = q_tiles.shape
    kv_cols = kv_tiles.shape[1]
    chunk = min(TILE, depth)
    return pl.pallas_call(
        rescale_kernel,
        grid=(depth // chunk,),
        in_specs=[
            pl.BlockSpec((chunk, q_cols), lambda i: (i, 0)),
            pl.BlockSpec((chunk, kv_cols), lambda i: (i, 0)),
            pl.BlockSpec(scales.shape, lambda i: (0, 0)),
        ],
        out_specs=IN_VMEM,
        out_shape=pltpu.VMEM((depth, q_cols + kv_cols), jnp.bfloat16),
        compiler_params=PARAMS,
        cost_estimate=cost(depth * (q_cols + kv_cols), 2 * depth * (q_cols + kv_cols)),
        name="rescale",
    )(in_hbm(q_tiles), in_hbm(kv_tiles), scales)


def fetch_kernel(source, target, done):
    parts = done.shape[0]
    rows = source.shape[0] // parts
    copies = []
    for part in range(parts):
        span = pl.ds(part * rows, rows)
        copies.append(pltpu.make_async_copy(source.at[span], target.at[span], done.at[part]))
    for copy in copies:
        copy.start()
    for copy in copies:
        copy.wait()


def fetch(weight):
    return pl.pallas_call(
        fetch_kernel,
        in_specs=[IN_HBM],
        out_specs=IN_VMEM,
        out_shape=pltpu.VMEM(weight.shape, weight.dtype),
        scratch_shapes=[pltpu.SemaphoreType.DMA((4,))],
        compiler_params=PARAMS,
        cost_estimate=cost(0, 2 * weight.size),
        name="fetch",
    )(in_hbm(weight))


def project_kernel(turns, pieces, natural, replicas, behind, last, place, *refs):
    count = len(turns)
    blocks, gain, weight = refs[:count], refs[count], refs[count + 1]
    rows, width = blocks[0].shape
    columns = weight.shape[1]
    total, held, result = refs[-2], refs[-1], refs[-3]
    if len(refs) == count + 6:
        total[...] = refs[count + 2][...]
    else:
        total[...] = jnp.zeros_like(total)
    wanted = lax.rem(place[0] + replicas - behind, replicas)

    def add(block, number):
        span = pl.ds(pl.multiple_of(number * width, HEAD), width)
        squares = []
        for start in range(0, rows, STRIP):
            values = block[start:start + STRIP, :].astype(jnp.float32)
            held[start:start + STRIP, :] = (values * gain[:, span]).astype(jnp.bfloat16)
            squares.append(jnp.sum(values * values, -1, keepdims=True))
        square = jnp.broadcast_to(jnp.concatenate(squares, 0), (rows, HEAD))
        total[:, columns:] += square
        for start, size in tiles_of(columns):
            product = jnp.dot(
                held[...], weight[span, start:start + size], preferred_element_type=jnp.float32
            )
            total[:, start:start + size] += product

    for turn, block in zip(turns, blocks):
        number = lax.rem(place[1] + pieces - turn, pieces)
        if natural:
            part = lax.div(number, replicas)
            pl.when(lax.rem(number, replicas) == wanted)(functools.partial(add, block, part))
        else:
            add(block, number)
    if last and behind:
        result[:, :columns] = total[:, :columns].astype(jnp.bfloat16)
        square = total[:, columns:]
        coarse = square.astype(jnp.bfloat16).astype(jnp.float32)
        lane = lax.broadcasted_iota(jnp.int32, square.shape, 1)
        result[:, columns:] = jnp.where(lane < HEAD // 2, coarse, square - coarse).astype(jnp.bfloat16)
    else:
        result[...] = total[...]


def project(turns, blocks, pieces, natural, replicas, behind, last, place, gain, weight, before):
    rows, width = blocks[0].shape
    columns = weight.shape[1] + HEAD
    kind = jnp.bfloat16 if last and behind else jnp.float32
    earlier = [] if before is None else [before]
    return pl.pallas_call(
        functools.partial(project_kernel, turns, pieces, natural, replicas, behind, last),
        in_specs=[IN_SMEM] + [IN_VMEM] * (len(blocks) + 2 + len(earlier)),
        out_specs=IN_VMEM,
        out_shape=jax.ShapeDtypeStruct((rows, columns), kind),
        scratch_shapes=[
            pltpu.VMEM((rows, columns), jnp.float32),
            pltpu.VMEM((rows, width), jnp.bfloat16),
        ],
        compiler_params=PARAMS,
        cost_estimate=cost(6 * len(blocks) * rows * width * columns, 2 * len(blocks) * width * columns),
        name="project",
    )(place, *blocks, gain, resident(weight), *earlier)


def attend_kernel(q_heads, kv_heads, features, length, own, *refs):
    received = refs[:-4]
    cosine, sine, out, cache = refs[-4:]
    rows = own.shape[0]
    group = q_heads // kv_heads

    def total(start):
        value = own[:, start:start + HEAD]
        for part in received:
            value = value + part[:, start:start + HEAD].astype(jnp.float32)
        return value

    tail = (q_heads + 2 * kv_heads) * HEAD
    square = own[:, tail:tail + 1]
    for part in received:
        pair = part[:, tail:].astype(jnp.float32)
        square = square + (pair[:, :1] + pair[:, HEAD // 2:HEAD // 2 + 1])
    factor = jnp.broadcast_to(lax.rsqrt(square / features + norm_eps), (rows, HEAD))

    def rotate(value):
        return value * cosine[...] + pltpu.roll(value, HEAD // 2, 1) * sine[...]

    row = lax.broadcasted_iota(jnp.int32, (rows, rows), 0)
    col = lax.broadcasted_iota(jnp.int32, (rows, rows), 1)
    mask = jnp.concatenate([(col <= row) & (col < length[0])] * group, 0)
    for kv_head in range(kv_heads):
        start = (q_heads + 2 * kv_head) * HEAD
        keys = rotate(total(start) * factor).astype(jnp.bfloat16)
        values = (total(start + HEAD) * factor).astype(jnp.bfloat16)
        cache[:, 2 * kv_head * HEAD:(2 * kv_head + 1) * HEAD] = keys
        cache[:, (2 * kv_head + 1) * HEAD:(2 * kv_head + 2) * HEAD] = values
        heads = range(kv_head * group, (kv_head + 1) * group)
        query = jnp.concatenate(
            [rotate(total(head * HEAD) * factor).astype(jnp.bfloat16) for head in heads], 0
        )
        scores = lax.dot_general(
            query, keys, (((1,), (1,)), ((), ())), preferred_element_type=jnp.float32
        )
        scores = jnp.where(mask, scores / jnp.sqrt(jnp.float32(HEAD)), -jnp.inf)
        expo = jnp.exp(scores - jnp.max(scores, -1, keepdims=True))
        probs = (expo / jnp.sum(expo, -1, keepdims=True)).astype(jnp.bfloat16)
        mixed = jnp.dot(probs, values, preferred_element_type=jnp.float32).astype(jnp.bfloat16)
        for number, head in enumerate(heads):
            out[:, head * HEAD:(head + 1) * HEAD] = mixed[number * rows:(number + 1) * rows, :]


def attend(own, received, length, cosine, sine, q_cols, kv_cols, features):
    rows = own.shape[0]
    return pl.pallas_call(
        functools.partial(attend_kernel, q_cols // HEAD, kv_cols // (2 * HEAD), features),
        in_specs=[IN_SMEM] + [IN_VMEM] * (3 + len(received)),
        out_specs=[IN_VMEM, IN_VMEM],
        out_shape=[
            jax.ShapeDtypeStruct((rows, q_cols), jnp.bfloat16),
            jax.ShapeDtypeStruct((rows, kv_cols), jnp.bfloat16),
        ],
        compiler_params=PARAMS,
        cost_estimate=cost(16 * rows * rows * q_cols, 6 * rows * (q_cols + kv_cols)),
        name="attend",
    )(length, own, *received, cosine, sine)


def spread_kernel(turn, shards, place, attended, weight, out):
    parts, _, width = out.shape
    goal = lax.rem(place[1] + turn, shards)
    for part in range(parts):
        if parts == 1:
            left = goal * width
        else:
            left = (lax.rem(place[0] + part, parts) * shards + goal) * width
        for start, size in tiles_of(width):
            span = pl.ds(pl.multiple_of(left + start, HEAD), size)
            product = jnp.dot(attended[...], weight[:, span], preferred_element_type=jnp.float32)
            out[part, :, start:start + size] = product.astype(jnp.bfloat16)


def spread(turn, shards, parts, place, attended, weight):
    rows, depth = attended.shape
    width = weight.shape[1] // (shards * parts)
    return pl.pallas_call(
        functools.partial(spread_kernel, turn, shards),
        in_specs=[IN_SMEM, IN_VMEM, IN_VMEM],
        out_specs=IN_VMEM,
        out_shape=jax.ShapeDtypeStruct((parts, rows, width), jnp.bfloat16),
        compiler_params=PARAMS,
        cost_estimate=cost(6 * rows * width * parts * depth, 2 * depth * width * parts),
        name="spread",
    )(place, attended, resident(weight))


def per_device(sizes, hidden_in, lengths, norm_gain, q_tiles, q_scales, kv_tiles, kv_scales, out_weight):
    replicas, sections, shards = sizes
    section = lax.axis_index("section")
    me, lane = lax.axis_index("replica"), lax.axis_index("tensor")
    rows, width = hidden_in.shape
    features = norm_gain.shape[1]
    q_tiles, kv_tiles = q_tiles[0], kv_tiles[0]
    depth, q_cols = q_tiles.shape
    kv_cols = kv_tiles.shape[1]
    per_slice = shards // replicas
    cell = width // replicas
    place = jnp.stack([me, lane]).astype(jnp.int32)
    gain = lax.dynamic_slice_in_dim(norm_gain, me * depth, depth, 1)
    scales = jnp.repeat(jnp.concatenate([q_scales[0], kv_scales[0]], 1).astype(jnp.float32), BLOCK, 1)
    half = HEAD // 2
    freq = rope_base ** (-jnp.arange(half, dtype=jnp.float32) / half)
    angle = jnp.arange(rows, dtype=jnp.float32)[:, None] * freq[None, :]
    cosine = jnp.concatenate([jnp.cos(angle)] * 2, 1)
    sine = jnp.concatenate([-jnp.sin(angle), jnp.sin(angle)], 1)
    w_in = rescale(q_tiles, kv_tiles, scales)
    w_out = fetch(lax.optimization_barrier((out_weight, w_in))[0][0])

    def device(replica, sect, shard):
        return (replica * sections + sect) * shards + shard

    def move(value, pair_of):
        pairs = []
        for replica in range(replicas):
            for shard in range(shards):
                source, target = pair_of(replica, shard)
                pairs.append((device(*source), device(*target)))
        return lax.ppermute(value, AXES, pairs)

    def move_in(value, layer, goal_of, ahead=0):
        pairs = []
        for sect in range(layer % 2, sections - ahead, 2):
            for replica in range(replicas):
                for shard in range(shards):
                    goal = goal_of(replica, shard)
                    pairs.append((device(replica, sect, shard), device(goal[0], sect + ahead, goal[1])))
        return lax.ppermute(value, AXES, pairs)

    def pick(values, index):
        return lax.dynamic_index_in_dim(jnp.stack(values), index, 0, keepdims=False)

    def interleave(value, origin, target):
        came = []
        for turn in range(replicas):
            start = lax.rem(lane // per_slice + turn, replicas) * cell
            came.append(
                move(
                    lax.dynamic_slice_in_dim(value, start, cell, 1),
                    lambda replica, shard: (
                        (replica, origin, shard),
                        (
                            replica,
                            target,
                            shard % per_slice * replicas + (shard // per_slice + turn) % replicas,
                        ),
                    ),
                )
            )
        return [pick(came, jnp.mod(lane - me - part, replicas)) for part in range(replicas)]

    def restore(cells, layer):
        came = []
        for turn in range(replicas):
            came.append(
                move_in(
                    pick(cells, jnp.mod(lane + turn - me, replicas)),
                    layer,
                    lambda replica, shard: (
                        replica,
                        (shard + turn) % replicas * per_slice + shard // replicas,
                    ),
                )
            )
        slots = [pick(came, jnp.mod(lane // per_slice - slot, replicas)) for slot in range(replicas)]
        return jnp.concatenate(slots, 1)

    def gather_natural(value):
        def pair_of(turn, replica, shard):
            goal = (shard % per_slice * replicas + replica + turn) % shards
            return (replica, turn % sections, shard), (shard // per_slice, 0, goal)

        return [move(value, functools.partial(pair_of, turn)) for turn in range(shards)]

    def gather_cells(value, part, layer):
        def goal_of(turn, replica, shard):
            return (replica + part) % replicas, (shard + turn) % shards

        return [move_in(value, layer, functools.partial(goal_of, turn), 1) for turn in far_first]

    far_first = sorted(range(shards), key=lambda turn: -min(turn, shards - turn))
    order = list(range(1, replicas)) + [0]
    layer_out, cache_out = None, None
    residual = interleave(hidden_in, sections - 1, 0)
    pieces = gather_natural(hidden_in)
    for layer in range(sections):
        final = layer == sections - 1
        received = []
        for behind in order:
            turns = list(range(shards)) if layer == 0 else far_first
            blocks = pieces if layer == 0 else pieces[behind]
            if received:
                blocks = lax.optimization_barrier((blocks, ready))[0]
            total = None
            if layer == 0:
                groups = [range(shards)]
            else:
                groups = [range(shards // 2), range(shards // 2, shards)]
            for group in groups:
                total = project(
                    [turns[i] for i in group],
                    [blocks[i] for i in group],
                    shards,
                    layer == 0,
                    replicas,
                    behind,
                    group is groups[-1],
                    place,
                    gain,
                    w_in,
                    total,
                )
            if behind:
                ready = total
                received.append(
                    move_in(
                        total,
                        layer,
                        lambda replica, shard: ((replica - behind) % replicas, shard),
                    )
                )
        attended, cache = attend(total, received, lengths, cosine, sine, q_cols, kv_cols, features)
        parts = 1 if final else replicas
        arrived = []
        for turn in far_first:
            partial = spread(turn, shards, parts, place, attended, w_out)
            if turn:
                partial = move_in(
                    partial, layer, lambda replica, shard: (replica, (shard + turn) % shards)
                )
            arrived.append(partial)
        result = []
        for part in range(parts):
            value = residual[part].astype(jnp.float32)
            for partial in arrived:
                value = value + partial[part].astype(jnp.float32)
            result.append(value.astype(jnp.bfloat16))
        if final:
            natural = result[0]
        else:
            pieces = {}
            for part in order:
                pieces[part] = gather_cells(result[part], part, layer)
            natural = restore(result, layer)
            along = lambda replica, shard: (replica, shard)
            if layer == sections - 2:
                residual = [move_in(natural, layer, along, 1)]
            else:
                residual = [move_in(value, layer, along, 1) for value in result]
        if layer == 0:
            layer_out, cache_out = natural, cache
        else:
            layer_out = jnp.where(section == layer, natural, layer_out)
            cache_out = jnp.where(section == layer, cache, cache_out)
        if not final:
            layer_out, cache_out = lax.optimization_barrier((layer_out, cache_out))
    return layer_out[None], cache_out[None]


def solution(mesh):
    sizes = tuple(mesh.shape[axis] for axis in AXES)
    in_specs = (
        P("replica", "tensor"),
        P("replica"),
        P("section", None),
        P("section", "replica", "tensor"),
        P("section", "replica", "tensor"),
        P("section", "replica", "tensor"),
        P("section", "replica", "tensor"),
        P("section", "tensor", None),
    )
    out_specs = (P("section", "replica", "tensor"), P("section", "replica", "tensor"))
    return jax.shard_map(
        functools.partial(per_device, sizes),
        mesh=mesh,
        in_specs=in_specs,
        out_specs=out_specs,
        check_vma=False,
    )
```

```python
import functools

import jax
import jax.numpy as jnp
from jax import lax
from jax.experimental import pallas as pl
from jax.experimental.pallas import tpu as pltpu
from jax.sharding import PartitionSpec as P

HEAD = 128
BLOCK = 128
STRIP = 16
TILE = 512

rope_base = 1000000.0
norm_eps = 1e-06

AXES = ("replica", "section", "tensor")
PARAMS = pltpu.CompilerParams(vmem_limit_bytes=8 * 1024 * 1024)
IN_VMEM = pl.BlockSpec(memory_space=pltpu.VMEM)
IN_SMEM = pl.BlockSpec(memory_space=pltpu.SMEM)
IN_HBM = pl.BlockSpec(memory_space=pl.ANY)


def cost(flops, moved):
    return pl.CostEstimate(flops=flops, bytes_accessed=moved, transcendentals=0)


def resident(value):
    return pltpu.with_memory_space_constraint(value, pltpu.VMEM)


def in_hbm(value):
    return pltpu.with_memory_space_constraint(value, pltpu.HBM)


def tiles_of(columns):
    return [(start, min(TILE, columns - start)) for start in range(0, columns, TILE)]


def rescale_kernel(q_tile, kv_tile, scale, out):
    step = pl.program_id(0)
    q_cols = q_tile.shape[1]
    chunk = q_tile.shape[0]
    for number in range(chunk // BLOCK):
        source = pl.ds(number * BLOCK, BLOCK)
        target = pl.ds(pl.multiple_of(step * chunk + number * BLOCK, BLOCK), BLOCK)
        line = scale[pl.ds(step * (chunk // BLOCK) + number, 1), :]
        for tile, left in ((q_tile, 0), (kv_tile, q_cols)):
            width = tile.shape[1]
            factor = jnp.broadcast_to(line[:, left:left + width], (BLOCK, width))
            value = tile[source, :].astype(jnp.float32) * factor
            out[target, left:left + width] = value.astype(jnp.bfloat16)


def rescale(q_tiles, kv_tiles, scales):
    depth, q_cols = q_tiles.shape
    kv_cols = kv_tiles.shape[1]
    chunk = min(TILE, depth)
    return pl.pallas_call(
        rescale_kernel,
        grid=(depth // chunk,),
        in_specs=[
            pl.BlockSpec((chunk, q_cols), lambda i: (i, 0)),
            pl.BlockSpec((chunk, kv_cols), lambda i: (i, 0)),
            pl.BlockSpec(scales.shape, lambda i: (0, 0)),
        ],
        out_specs=IN_VMEM,
        out_shape=pltpu.VMEM((depth, q_cols + kv_cols), jnp.bfloat16),
        compiler_params=PARAMS,
        cost_estimate=cost(depth * (q_cols + kv_cols), 2 * depth * (q_cols + kv_cols)),
        name="rescale",
    )(in_hbm(q_tiles), in_hbm(kv_tiles), scales)


def fetch_kernel(source, target, done):
    parts = done.shape[0]
    rows = source.shape[0] // parts
    copies = []
    for part in range(parts):
        span = pl.ds(part * rows, rows)
        copies.append(pltpu.make_async_copy(source.at[span], target.at[span], done.at[part]))
    for copy in copies:
        copy.start()
    for copy in copies:
        copy.wait()


def fetch(weight):
    return pl.pallas_call(
        fetch_kernel,
        in_specs=[IN_HBM],
        out_specs=IN_VMEM,
        out_shape=pltpu.VMEM(weight.shape, weight.dtype),
        scratch_shapes=[pltpu.SemaphoreType.DMA((4,))],
        compiler_params=PARAMS,
        cost_estimate=cost(0, 2 * weight.size),
        name="fetch",
    )(in_hbm(weight))


def project_kernel(turns, pieces, natural, replicas, behind, last, place, *refs):
    count = len(turns)
    blocks, gain, weight = refs[:count], refs[count], refs[count + 1]
    rows, width = blocks[0].shape
    columns = weight.shape[1]
    total, held, result = refs[-2], refs[-1], refs[-3]
    if len(refs) == count + 6:
        total[...] = refs[count + 2][...]
    else:
        total[...] = jnp.zeros_like(total)
    wanted = lax.rem(place[0] + replicas - behind, replicas)

    def add(block, number):
        span = pl.ds(pl.multiple_of(number * width, HEAD), width)
        squares = []
        for start in range(0, rows, STRIP):
            values = block[start:start + STRIP, :].astype(jnp.float32)
            held[start:start + STRIP, :] = (values * gain[:, span]).astype(jnp.bfloat16)
            squares.append(jnp.sum(values * values, -1, keepdims=True))
        square = jnp.broadcast_to(jnp.concatenate(squares, 0), (rows, HEAD))
        total[:, columns:] += square
        for start, size in tiles_of(columns):
            product = jnp.dot(
                held[...], weight[span, start:start + size], preferred_element_type=jnp.float32
            )
            total[:, start:start + size] += product

    for turn, block in zip(turns, blocks):
        number = lax.rem(place[1] + pieces - turn, pieces)
        if natural:
            part = lax.div(number, replicas)
            pl.when(lax.rem(number, replicas) == wanted)(functools.partial(add, block, part))
        else:
            add(block, number)
    if last and behind:
        result[:, :columns] = total[:, :columns].astype(jnp.bfloat16)
        square = total[:, columns:]
        coarse = square.astype(jnp.bfloat16).astype(jnp.float32)
        lane = lax.broadcasted_iota(jnp.int32, square.shape, 1)
        result[:, columns:] = jnp.where(lane < HEAD // 2, coarse, square - coarse).astype(jnp.bfloat16)
    else:
        result[...] = total[...]


def project(turns, blocks, pieces, natural, replicas, behind, last, place, gain, weight, before):
    rows, width = blocks[0].shape
    columns = weight.shape[1] + HEAD
    kind = jnp.bfloat16 if last and behind else jnp.float32
    earlier = [] if before is None else [before]
    return pl.pallas_call(
        functools.partial(project_kernel, turns, pieces, natural, replicas, behind, last),
        in_specs=[IN_SMEM] + [IN_VMEM] * (len(blocks) + 2 + len(earlier)),
        out_specs=IN_VMEM,
        out_shape=jax.ShapeDtypeStruct((rows, columns), kind),
        scratch_shapes=[
            pltpu.VMEM((rows, columns), jnp.float32),
            pltpu.VMEM((rows, width), jnp.bfloat16),
        ],
        compiler_params=PARAMS,
        cost_estimate=cost(6 * len(blocks) * rows * width * columns, 2 * len(blocks) * width * columns),
        name="project",
    )(place, *blocks, gain, resident(weight), *earlier)


def attend_kernel(q_heads, kv_heads, features, length, own, *refs):
    received = refs[:-4]
    cosine, sine, out, cache = refs[-4:]
    rows = own.shape[0]
    group = q_heads // kv_heads

    def total(start):
        value = own[:, start:start + HEAD]
        for part in received:
            value = value + part[:, start:start + HEAD].astype(jnp.float32)
        return value

    tail = (q_heads + 2 * kv_heads) * HEAD
    square = own[:, tail:tail + 1]
    for part in received:
        pair = part[:, tail:].astype(jnp.float32)
        square = square + (pair[:, :1] + pair[:, HEAD // 2:HEAD // 2 + 1])
    factor = jnp.broadcast_to(lax.rsqrt(square / features + norm_eps), (rows, HEAD))

    def rotate(value):
        return value * cosine[...] + pltpu.roll(value, HEAD // 2, 1) * sine[...]

    row = lax.broadcasted_iota(jnp.int32, (rows, rows), 0)
    col = lax.broadcasted_iota(jnp.int32, (rows, rows), 1)
    mask = jnp.concatenate([(col <= row) & (col < length[0])] * group, 0)
    for kv_head in range(kv_heads):
        start = (q_heads + 2 * kv_head) * HEAD
        keys = rotate(total(start) * factor).astype(jnp.bfloat16)
        values = (total(start + HEAD) * factor).astype(jnp.bfloat16)
        cache[:, 2 * kv_head * HEAD:(2 * kv_head + 1) * HEAD] = keys
        cache[:, (2 * kv_head + 1) * HEAD:(2 * kv_head + 2) * HEAD] = values
        heads = range(kv_head * group, (kv_head + 1) * group)
        query = jnp.concatenate(
            [rotate(total(head * HEAD) * factor).astype(jnp.bfloat16) for head in heads], 0
        )
        scores = lax.dot_general(
            query, keys, (((1,), (1,)), ((), ())), preferred_element_type=jnp.float32
        )
        scores = jnp.where(mask, scores / jnp.sqrt(jnp.float32(HEAD)), -jnp.inf)
        expo = jnp.exp(scores - jnp.max(scores, -1, keepdims=True))
        probs = (expo / jnp.sum(expo, -1, keepdims=True)).astype(jnp.bfloat16)
        mixed = jnp.dot(probs, values, preferred_element_type=jnp.float32).astype(jnp.bfloat16)
        for number, head in enumerate(heads):
            out[:, head * HEAD:(head + 1) * HEAD] = mixed[number * rows:(number + 1) * rows, :]


def attend(own, received, length, cosine, sine, q_cols, kv_cols, features):
    rows = own.shape[0]
    return pl.pallas_call(
        functools.partial(attend_kernel, q_cols // HEAD, kv_cols // (2 * HEAD), features),
        in_specs=[IN_SMEM] + [IN_VMEM] * (3 + len(received)),
        out_specs=[IN_VMEM, IN_VMEM],
        out_shape=[
            jax.ShapeDtypeStruct((rows, q_cols), jnp.bfloat16),
            jax.ShapeDtypeStruct((rows, kv_cols), jnp.bfloat16),
        ],
        compiler_params=PARAMS,
        cost_estimate=cost(16 * rows * rows * q_cols, 6 * rows * (q_cols + kv_cols)),
        name="attend",
    )(length, own, *received, cosine, sine)


def spread_kernel(turn, shards, place, attended, weight, out):
    parts, _, width = out.shape
    goal = lax.rem(place[1] + turn, shards)
    for part in range(parts):
        if parts == 1:
            left = goal * width
        else:
            left = (lax.rem(place[0] + part, parts) * shards + goal) * width
        for start, size in tiles_of(width):
            span = pl.ds(pl.multiple_of(left + start, HEAD), size)
            product = jnp.dot(attended[...], weight[:, span], preferred_element_type=jnp.float32)
            out[part, :, start:start + size] = product.astype(jnp.bfloat16)


def spread(turn, shards, parts, place, attended, weight):
    rows, depth = attended.shape
    width = weight.shape[1] // (shards * parts)
    return pl.pallas_call(
        functools.partial(spread_kernel, turn, shards),
        in_specs=[IN_SMEM, IN_VMEM, IN_VMEM],
        out_specs=IN_VMEM,
        out_shape=jax.ShapeDtypeStruct((parts, rows, width), jnp.bfloat16),
        compiler_params=PARAMS,
        cost_estimate=cost(6 * rows * width * parts * depth, 2 * depth * width * parts),
        name="spread",
    )(place, attended, resident(weight))


def per_device(sizes, hidden_in, lengths, norm_gain, q_tiles, q_scales, kv_tiles, kv_scales, out_weight):
    replicas, sections, shards = sizes
    section = lax.axis_index("section")
    me, lane = lax.axis_index("replica"), lax.axis_index("tensor")
    rows, width = hidden_in.shape
    features = norm_gain.shape[1]
    q_tiles, kv_tiles = q_tiles[0], kv_tiles[0]
    depth, q_cols = q_tiles.shape
    kv_cols = kv_tiles.shape[1]
    per_slice = shards // replicas
    cell = width // replicas
    place = jnp.stack([me, lane]).astype(jnp.int32)
    gain = lax.dynamic_slice_in_dim(norm_gain, me * depth, depth, 1)
    scales = jnp.repeat(jnp.concatenate([q_scales[0], kv_scales[0]], 1).astype(jnp.float32), BLOCK, 1)
    half = HEAD // 2
    freq = rope_base ** (-jnp.arange(half, dtype=jnp.float32) / half)
    angle = jnp.arange(rows, dtype=jnp.float32)[:, None] * freq[None, :]
    cosine = jnp.concatenate([jnp.cos(angle)] * 2, 1)
    sine = jnp.concatenate([-jnp.sin(angle), jnp.sin(angle)], 1)
    numbers = {"shift": lane - me, "slice": lane // per_slice}
    which = {name: [jnp.mod(number, replicas) == i for i in range(replicas)] for name, number in numbers.items()}
    at = [section == layer for layer in range(sections)]
    scales, gain, cosine, sine, place, which, at, lengths = lax.optimization_barrier(
        (scales, gain, cosine, sine, place, which, at, lengths)
    )
    w_in = rescale(q_tiles, kv_tiles, scales)
    w_out = fetch(lax.optimization_barrier((out_weight, w_in))[0][0])

    def pick(values, name, plus=0):
        found = values[plus % replicas]
        for number in range(1, replicas):
            found = jnp.where(which[name][number], values[(plus + number) % replicas], found)
        return found

    def device(replica, sect, shard):
        return (replica * sections + sect) * shards + shard

    def move(value, pair_of):
        pairs = []
        for replica in range(replicas):
            for shard in range(shards):
                source, target = pair_of(replica, shard)
                pairs.append((device(*source), device(*target)))
        return lax.ppermute(value, AXES, pairs)

    def move_in(value, layer, goal_of, ahead=0):
        pairs = []
        for sect in range(layer % 2, sections - ahead, 2):
            for replica in range(replicas):
                for shard in range(shards):
                    goal = goal_of(replica, shard)
                    pairs.append((device(replica, sect, shard), device(goal[0], sect + ahead, goal[1])))
        return lax.ppermute(value, AXES, pairs)

    def interleave(value, origin, target):
        came = []
        for turn in range(replicas):
            came.append(
                move(
                    pick([value[:, i * cell:(i + 1) * cell] for i in range(replicas)], "slice", turn),
                    lambda replica, shard: (
                        (replica, origin, shard),
                        (
                            replica,
                            target,
                            shard % per_slice * replicas + (shard // per_slice + turn) % replicas,
                        ),
                    ),
                )
            )
        return [pick(came, "shift", -part) for part in range(replicas)]

    def restore(cells, layer):
        came = []
        for turn in range(replicas):
            came.append(
                move_in(
                    pick(cells, "shift", turn),
                    layer,
                    lambda replica, shard: (
                        replica,
                        (shard + turn) % replicas * per_slice + shard // replicas,
                    ),
                )
            )
        slots = [pick(came, "slice", -slot) for slot in range(replicas)]
        return jnp.concatenate(slots, 1)

    def gather_natural(value):
        def pair_of(turn, replica, shard):
            goal = (shard % per_slice * replicas + replica + turn) % shards
            return (replica, turn % sections, shard), (shard // per_slice, 0, goal)

        return [move(value, functools.partial(pair_of, turn)) for turn in range(shards)]

    def gather_cells(value, part, layer):
        def goal_of(turn, replica, shard):
            return (replica + part) % replicas, (shard + turn) % shards

        return [move_in(value, layer, functools.partial(goal_of, turn), 1) for turn in far_first]

    far_first = sorted(range(shards), key=lambda turn: -min(turn, shards - turn))
    order = list(range(1, replicas)) + [0]
    layer_out, cache_out = None, None
    residual = interleave(hidden_in, sections - 1, 0)
    pieces = gather_natural(hidden_in)
    for layer in range(sections):
        final = layer == sections - 1
        received = []
        for behind in order:
            turns = list(range(shards)) if layer == 0 else far_first
            blocks = pieces if layer == 0 else pieces[behind]
            if received:
                blocks = lax.optimization_barrier((blocks, ready))[0]
            total = None
            if layer == 0:
                groups = [range(shards)]
            else:
                groups = [range(shards // 2), range(shards // 2, shards)]
            for group in groups:
                total = project(
                    [turns[i] for i in group],
                    [blocks[i] for i in group],
                    shards,
                    layer == 0,
                    replicas,
                    behind,
                    group is groups[-1],
                    place,
                    gain,
                    w_in,
                    total,
                )
            if behind:
                ready = total
                received.append(
                    move_in(
                        total,
                        layer,
                        lambda replica, shard: ((replica - behind) % replicas, shard),
                    )
                )
        attended, cache = attend(total, received, lengths, cosine, sine, q_cols, kv_cols, features)
        parts = 1 if final else replicas
        arrived = []
        for turn in far_first:
            partial = spread(turn, shards, parts, place, attended, w_out)
            if turn:
                partial = move_in(
                    partial, layer, lambda replica, shard: (replica, (shard + turn) % shards)
                )
            arrived.append(partial)
        result = []
        for part in range(parts):
            value = residual[part].astype(jnp.float32)
            for partial in arrived:
                value = value + partial[part].astype(jnp.float32)
            result.append(value.astype(jnp.bfloat16))
        if final:
            natural = result[0]
        else:
            pieces = {}
            for part in order:
                pieces[part] = gather_cells(result[part], part, layer)
            natural = restore(result, layer)
            along = lambda replica, shard: (replica, shard)
            if layer == sections - 2:
                residual = [move_in(natural, layer, along, 1)]
            else:
                residual = [move_in(value, layer, along, 1) for value in result]
        if layer == 0:
            layer_out, cache_out = natural, cache
        else:
            layer_out = jnp.where(at[layer], natural, layer_out)
            cache_out = jnp.where(at[layer], cache, cache_out)
        if not final:
            layer_out, cache_out = lax.optimization_barrier((layer_out, cache_out))
    return layer_out[None], cache_out[None]


def solution(mesh):
    sizes = tuple(mesh.shape[axis] for axis in AXES)
    in_specs = (
        P("replica", "tensor"),
        P("replica"),
        P("section", None),
        P("section", "replica", "tensor"),
        P("section", "replica", "tensor"),
        P("section", "replica", "tensor"),
        P("section", "replica", "tensor"),
        P("section", "tensor", None),
    )
    out_specs = (P("section", "replica", "tensor"), P("section", "replica", "tensor"))
    return jax.shard_map(
        functools.partial(per_device, sizes),
        mesh=mesh,
        in_specs=in_specs,
        out_specs=out_specs,
        check_vma=False,
    )
```

```python
import functools

import jax
import jax.numpy as jnp
from jax import lax
from jax.experimental import pallas as pl
from jax.experimental.pallas import tpu as pltpu
from jax.sharding import PartitionSpec as P

HEAD = 128
BLOCK = 128
STRIP = 16
TILE = 512
CHUNKS = 2

rope_base = 1000000.0
norm_eps = 1e-06

AXES = ("replica", "section", "tensor")
PARAMS = pltpu.CompilerParams(vmem_limit_bytes=8 * 1024 * 1024)
IN_VMEM = pl.BlockSpec(memory_space=pltpu.VMEM)
IN_SMEM = pl.BlockSpec(memory_space=pltpu.SMEM)
IN_HBM = pl.BlockSpec(memory_space=pl.ANY)


def cost(flops, moved):
    return pl.CostEstimate(flops=flops, bytes_accessed=moved, transcendentals=0)


def resident(value):
    return pltpu.with_memory_space_constraint(value, pltpu.VMEM)


def in_hbm(value):
    return pltpu.with_memory_space_constraint(value, pltpu.HBM)


def tiles_of(columns):
    return [(start, min(TILE, columns - start)) for start in range(0, columns, TILE)]


def rescale_kernel(q_tile, kv_tile, scale, out):
    step = pl.program_id(0)
    q_cols = q_tile.shape[1]
    chunk = q_tile.shape[0]
    for number in range(chunk // BLOCK):
        source = pl.ds(number * BLOCK, BLOCK)
        target = pl.ds(pl.multiple_of(step * chunk + number * BLOCK, BLOCK), BLOCK)
        line = scale[pl.ds(step * (chunk // BLOCK) + number, 1), :]
        for tile, left in ((q_tile, 0), (kv_tile, q_cols)):
            width = tile.shape[1]
            factor = jnp.broadcast_to(line[:, left:left + width], (BLOCK, width))
            value = tile[source, :].astype(jnp.float32) * factor
            out[target, left:left + width] = value.astype(jnp.bfloat16)


def rescale(q_tiles, kv_tiles, scales):
    depth, q_cols = q_tiles.shape
    kv_cols = kv_tiles.shape[1]
    chunk = min(TILE, depth)
    return pl.pallas_call(
        rescale_kernel,
        grid=(depth // chunk,),
        in_specs=[
            pl.BlockSpec((chunk, q_cols), lambda i: (i, 0)),
            pl.BlockSpec((chunk, kv_cols), lambda i: (i, 0)),
            pl.BlockSpec(scales.shape, lambda i: (0, 0)),
        ],
        out_specs=IN_VMEM,
        out_shape=pltpu.VMEM((depth, q_cols + kv_cols), jnp.bfloat16),
        compiler_params=PARAMS,
        cost_estimate=cost(depth * (q_cols + kv_cols), 2 * depth * (q_cols + kv_cols)),
        name="rescale",
    )(in_hbm(q_tiles), in_hbm(kv_tiles), scales)


def fetch_kernel(source, target, done):
    parts = done.shape[0]
    rows = source.shape[0] // parts
    copies = []
    for part in range(parts):
        span = pl.ds(part * rows, rows)
        copies.append(pltpu.make_async_copy(source.at[span], target.at[span], done.at[part]))
    for copy in copies:
        copy.start()
    for copy in copies:
        copy.wait()


def fetch(weight):
    return pl.pallas_call(
        fetch_kernel,
        in_specs=[IN_HBM],
        out_specs=IN_VMEM,
        out_shape=pltpu.VMEM(weight.shape, weight.dtype),
        scratch_shapes=[pltpu.SemaphoreType.DMA((4,))],
        compiler_params=PARAMS,
        cost_estimate=cost(0, 2 * weight.size),
        name="fetch",
    )(in_hbm(weight))


def project_kernel(turns, pieces, stride, offset, replicas, behind, last, place, *refs):
    count = len(turns)
    blocks, gain, weight = refs[:count], refs[count], refs[count + 1]
    rows, width = blocks[0].shape
    columns = weight.shape[1]
    total, held, result = refs[-2], refs[-1], refs[-3]
    if len(refs) == count + 6:
        total[...] = refs[count + 2][...]
    else:
        total[...] = jnp.zeros_like(total)
    wanted = lax.rem(place[0] + replicas - behind, replicas)

    def add(block, part):
        span = pl.ds(pl.multiple_of(part * stride + offset, HEAD), width)
        squares = []
        for start in range(0, rows, STRIP):
            values = block[start:start + STRIP, :].astype(jnp.float32)
            held[start:start + STRIP, :] = (values * gain[:, span]).astype(jnp.bfloat16)
            squares.append(jnp.sum(values * values, -1, keepdims=True))
        square = jnp.broadcast_to(jnp.concatenate(squares, 0), (rows, HEAD))
        total[:, columns:] += square
        for start, size in tiles_of(columns):
            product = jnp.dot(
                held[...], weight[span, start:start + size], preferred_element_type=jnp.float32
            )
            total[:, start:start + size] += product

    for turn, block in zip(turns, blocks):
        number = lax.rem(place[1] + pieces - turn, pieces)
        part = lax.div(number, replicas)
        pl.when(lax.rem(number, replicas) == wanted)(functools.partial(add, block, part))
    if last and behind:
        result[:, :columns] = total[:, :columns].astype(jnp.bfloat16)
        square = total[:, columns:]
        coarse = square.astype(jnp.bfloat16).astype(jnp.float32)
        lane = lax.broadcasted_iota(jnp.int32, square.shape, 1)
        result[:, columns:] = jnp.where(lane < HEAD // 2, coarse, square - coarse).astype(jnp.bfloat16)
    else:
        result[...] = total[...]


def project(turns, blocks, stride, offset, replicas, behind, last, place, gain, weight, before):
    rows, width = blocks[0].shape
    columns = weight.shape[1] + HEAD
    kind = jnp.bfloat16 if last and behind else jnp.float32
    earlier = [] if before is None else [before]
    return pl.pallas_call(
        functools.partial(project_kernel, turns, len(turns), stride, offset, replicas, behind, last),
        in_specs=[IN_SMEM] + [IN_VMEM] * (len(blocks) + 2 + len(earlier)),
        out_specs=IN_VMEM,
        out_shape=jax.ShapeDtypeStruct((rows, columns), kind),
        scratch_shapes=[
            pltpu.VMEM((rows, columns), jnp.float32),
            pltpu.VMEM((rows, width), jnp.bfloat16),
        ],
        compiler_params=PARAMS,
        cost_estimate=cost(
            6 * len(blocks) // replicas * rows * width * columns, 2 * len(blocks) * width * columns
        ),
        name="project",
    )(place, *blocks, gain, resident(weight), *earlier)


def attend_kernel(q_heads, kv_heads, features, length, own, *refs):
    received = refs[:-4]
    cosine, sine, out, cache = refs[-4:]
    rows = own.shape[0]
    group = q_heads // kv_heads

    def total(start):
        value = own[:, start:start + HEAD]
        for part in received:
            value = value + part[:, start:start + HEAD].astype(jnp.float32)
        return value

    tail = (q_heads + 2 * kv_heads) * HEAD
    square = own[:, tail:tail + 1]
    for part in received:
        pair = part[:, tail:].astype(jnp.float32)
        square = square + (pair[:, :1] + pair[:, HEAD // 2:HEAD // 2 + 1])
    factor = jnp.broadcast_to(lax.rsqrt(square / features + norm_eps), (rows, HEAD))

    def rotate(value):
        return value * cosine[...] + pltpu.roll(value, HEAD // 2, 1) * sine[...]

    row = lax.broadcasted_iota(jnp.int32, (rows, rows), 0)
    col = lax.broadcasted_iota(jnp.int32, (rows, rows), 1)
    mask = jnp.concatenate([(col <= row) & (col < length[0])] * group, 0)
    for kv_head in range(kv_heads):
        start = (q_heads + 2 * kv_head) * HEAD
        keys = rotate(total(start) * factor).astype(jnp.bfloat16)
        values = (total(start + HEAD) * factor).astype(jnp.bfloat16)
        cache[:, 2 * kv_head * HEAD:(2 * kv_head + 1) * HEAD] = keys
        cache[:, (2 * kv_head + 1) * HEAD:(2 * kv_head + 2) * HEAD] = values
        heads = range(kv_head * group, (kv_head + 1) * group)
        query = jnp.concatenate(
            [rotate(total(head * HEAD) * factor).astype(jnp.bfloat16) for head in heads], 0
        )
        scores = lax.dot_general(
            query, keys, (((1,), (1,)), ((), ())), preferred_element_type=jnp.float32
        )
        scores = jnp.where(mask, scores / jnp.sqrt(jnp.float32(HEAD)), -jnp.inf)
        expo = jnp.exp(scores - jnp.max(scores, -1, keepdims=True))
        probs = (expo / jnp.sum(expo, -1, keepdims=True)).astype(jnp.bfloat16)
        mixed = jnp.dot(probs, values, preferred_element_type=jnp.float32).astype(jnp.bfloat16)
        for number, head in enumerate(heads):
            out[:, head * HEAD:(head + 1) * HEAD] = mixed[number * rows:(number + 1) * rows, :]


def attend(own, received, length, cosine, sine, q_cols, kv_cols, features):
    rows = own.shape[0]
    return pl.pallas_call(
        functools.partial(attend_kernel, q_cols // HEAD, kv_cols // (2 * HEAD), features),
        in_specs=[IN_SMEM] + [IN_VMEM] * (3 + len(received)),
        out_specs=[IN_VMEM, IN_VMEM],
        out_shape=[
            jax.ShapeDtypeStruct((rows, q_cols), jnp.bfloat16),
            jax.ShapeDtypeStruct((rows, kv_cols), jnp.bfloat16),
        ],
        compiler_params=PARAMS,
        cost_estimate=cost(16 * rows * rows * q_cols, 6 * rows * (q_cols + kv_cols)),
        name="attend",
    )(length, own, *received, cosine, sine)


def spread_kernel(turn, shards, chunks, chunk, place, attended, weight, out):
    width = out.shape[1]
    goal = lax.rem(place[1] + turn, shards)
    for start, size in tiles_of(width):
        span = pl.ds(pl.multiple_of((goal * chunks + chunk) * width + start, HEAD), size)
        product = jnp.dot(attended[...], weight[:, span], preferred_element_type=jnp.float32)
        out[:, start:start + size] = product.astype(jnp.bfloat16)


def spread(turn, shards, chunks, chunk, place, attended, weight):
    rows, depth = attended.shape
    width = weight.shape[1] // (shards * chunks)
    return pl.pallas_call(
        functools.partial(spread_kernel, turn, shards, chunks, chunk),
        in_specs=[IN_SMEM, IN_VMEM, IN_VMEM],
        out_specs=IN_VMEM,
        out_shape=jax.ShapeDtypeStruct((rows, width), jnp.bfloat16),
        compiler_params=PARAMS,
        cost_estimate=cost(6 * rows * width * depth, 2 * depth * width),
        name="spread",
    )(place, attended, resident(weight))


def per_device(sizes, hidden_in, lengths, norm_gain, q_tiles, q_scales, kv_tiles, kv_scales, out_weight):
    replicas, sections, shards = sizes
    section = lax.axis_index("section")
    me, lane = lax.axis_index("replica"), lax.axis_index("tensor")
    rows, width = hidden_in.shape
    features = norm_gain.shape[1]
    q_tiles, kv_tiles = q_tiles[0], kv_tiles[0]
    depth, q_cols = q_tiles.shape
    kv_cols = kv_tiles.shape[1]
    per_slice = shards // replicas
    piece = width // CHUNKS
    place = jnp.stack([me, lane]).astype(jnp.int32)
    gain = lax.dynamic_slice_in_dim(norm_gain, me * depth, depth, 1)
    scales = jnp.repeat(jnp.concatenate([q_scales[0], kv_scales[0]], 1).astype(jnp.float32), BLOCK, 1)
    half = HEAD // 2
    freq = rope_base ** (-jnp.arange(half, dtype=jnp.float32) / half)
    angle = jnp.arange(rows, dtype=jnp.float32)[:, None] * freq[None, :]
    cosine = jnp.concatenate([jnp.cos(angle)] * 2, 1)
    sine = jnp.concatenate([-jnp.sin(angle), jnp.sin(angle)], 1)
    at = [section == layer for layer in range(sections)]
    scales, gain, cosine, sine, place, at, lengths = lax.optimization_barrier(
        (scales, gain, cosine, sine, place, at, lengths)
    )
    w_in = rescale(q_tiles, kv_tiles, scales)
    w_out = fetch(lax.optimization_barrier((out_weight, w_in))[0][0])

    def move(value, ways, goal_of):
        pairs = []
        for source, target in ways:
            for replica in range(replicas):
                for shard in range(shards):
                    ahead, beside = goal_of(replica, shard)
                    pairs.append(
                        (
                            (replica * sections + source) * shards + shard,
                            (ahead * sections + target) * shards + beside,
                        )
                    )
        return lax.ppermute(value, AXES, pairs)

    def after(value, earlier):
        return lax.optimization_barrier((value, earlier))[0]

    def same(replica, shard):
        return replica, shard

    def shifted(turn):
        return lambda replica, shard: (replica, (shard + turn) % shards)

    def to_slice(turn):
        return lambda replica, shard: (
            shard // per_slice,
            (shard % per_slice * replicas + replica + turn) % shards,
        )

    far_first = sorted(range(shards), key=lambda turn: -min(turn, shards - turn))
    turns = list(range(shards))
    order = list(range(1, replicas)) + [0]
    last = sections - 1
    helper = [last] * (sections - 2) + [sections - 3]
    back = {layer: [(helper[layer], layer)] for layer in range(last)}
    back[0] = back[last - 1] = [(helper[0], 0), (helper[last - 1], last - 1)]
    pieces = [[move(hidden_in, [(turn % sections, 0)], to_slice(turn)) for turn in turns]]
    held, layer_out, cache_out = hidden_in, hidden_in, None
    for layer in range(sections):
        twins = [(sect, sect) for sect in range(layer % 2, sections, 2)]
        totals, received = {}, []
        for number, blocks in enumerate(pieces):
            done = number == len(pieces) - 1
            for behind in order:
                if received:
                    blocks = lax.optimization_barrier((blocks, ready))[0]
                total = project(
                    turns,
                    blocks,
                    width,
                    number * blocks[0].shape[1],
                    replicas,
                    behind,
                    done,
                    place,
                    gain,
                    w_in,
                    totals.get(behind),
                )
                totals[behind] = total
                if done and behind:
                    ready = total
                    goal = lambda replica, shard: ((replica - behind) % replicas, shard)
                    received.append(move(total, twins, goal))
        attended, cache = attend(totals[0], received, lengths, cosine, sine, q_cols, kv_cols, features)
        if layer == last:
            value = residual.astype(jnp.float32)
            for turn in far_first:
                partial = spread(turn, shards, 1, 0, place, attended, w_out)
                if turn:
                    partial = move(partial, [(layer, layer)], shifted(turn))
                value = value + partial.astype(jnp.float32)
            result = value.astype(jnp.bfloat16)
        else:
            before = held if layer < last - 1 else layer_out
            pieces, results, summands = [], [], None
            for chunk in range(CHUNKS):
                start = before[:, chunk * piece:(chunk + 1) * piece]
                given = [attended] * shards
                if chunk:
                    start = after(start, results[-1])
                    given = [after(attended, partial) for partial in summands]
                partials = [
                    spread(turn, shards, CHUNKS, chunk, place, value, w_out)
                    for turn, value in zip(far_first, given)
                ]
                summands = [
                    move(partial, [(layer, helper[layer])], shifted(turn))
                    for turn, partial in zip(far_first, partials)
                ]
                value = start.astype(jnp.float32)
                for partial in summands:
                    value = value + partial.astype(jnp.float32)
                value = value.astype(jnp.bfloat16)
                copies = [value] * shards
                if chunk:
                    copies = [after(value, blocks) for blocks in pieces[-1]]
                ways = [(helper[layer], layer + 1)]
                pieces.append([move(copy, ways, to_slice(turn)) for turn, copy in zip(turns, copies)])
                results.append(value)
            held = jnp.concatenate(results, 1)
            result = move(held, back[layer], same)
            if layer == last - 1:
                residual = move(held, [(helper[layer], last)], same)
        if layer == 0:
            layer_out, cache_out = result, cache
        else:
            layer_out = jnp.where(at[layer], result, layer_out)
            cache_out = jnp.where(at[layer], cache, cache_out)
        if layer < last:
            layer_out, cache_out = lax.optimization_barrier((layer_out, cache_out))
    return layer_out[None], cache_out[None]


def solution(mesh):
    sizes = tuple(mesh.shape[axis] for axis in AXES)
    in_specs = (
        P("replica", "tensor"),
        P("replica"),
        P("section", None),
        P("section", "replica", "tensor"),
        P("section", "replica", "tensor"),
        P("section", "replica", "tensor"),
        P("section", "replica", "tensor"),
        P("section", "tensor", None),
    )
    out_specs = (P("section", "replica", "tensor"), P("section", "replica", "tensor"))
    return jax.shard_map(
        functools.partial(per_device, sizes),
        mesh=mesh,
        in_specs=in_specs,
        out_specs=out_specs,
        check_vma=False,
    )
```

```python
import functools

import jax
import jax.numpy as jnp
from jax import lax
from jax.experimental import pallas as pl
from jax.experimental.pallas import tpu as pltpu
from jax.sharding import PartitionSpec as P

HEAD = 128
BLOCK = 128
STRIP = 16
TILE = 512
CHUNKS = 2

rope_base = 1000000.0
norm_eps = 1e-06

AXES = ("replica", "section", "tensor")
PARAMS = pltpu.CompilerParams(vmem_limit_bytes=8 * 1024 * 1024)
IN_VMEM = pl.BlockSpec(memory_space=pltpu.VMEM)
IN_SMEM = pl.BlockSpec(memory_space=pltpu.SMEM)
IN_HBM = pl.BlockSpec(memory_space=pl.ANY)


def cost(flops, moved):
    return pl.CostEstimate(flops=flops, bytes_accessed=moved, transcendentals=0)


def resident(value):
    return pltpu.with_memory_space_constraint(value, pltpu.VMEM)


def in_hbm(value):
    return pltpu.with_memory_space_constraint(value, pltpu.HBM)


def tiles_of(columns):
    return [(start, min(TILE, columns - start)) for start in range(0, columns, TILE)]


def weights_kernel(q_tile, kv_tile, scale, source, out, target, done):
    step = pl.program_id(0)
    q_cols = q_tile.shape[1]
    chunk = q_tile.shape[0]
    parts = done.shape[0]
    depth = source.shape[0] // parts
    copies = []
    for part in range(parts):
        span = pl.ds(part * depth, depth)
        copies.append(pltpu.make_async_copy(source.at[span], target.at[span], done.at[part]))

    @pl.when(step == 0)
    def _():
        for copy in copies:
            copy.start()

    for number in range(chunk // BLOCK):
        rows = pl.ds(number * BLOCK, BLOCK)
        goal = pl.ds(pl.multiple_of(step * chunk + number * BLOCK, BLOCK), BLOCK)
        line = scale[pl.ds(step * (chunk // BLOCK) + number, 1), :]
        for tile, left in ((q_tile, 0), (kv_tile, q_cols)):
            width = tile.shape[1]
            factor = jnp.broadcast_to(line[:, left:left + width], (BLOCK, width))
            value = tile[rows, :].astype(jnp.float32) * factor
            out[goal, left:left + width] = value.astype(jnp.bfloat16)

    @pl.when(step == pl.num_programs(0) - 1)
    def _():
        for copy in copies:
            copy.wait()


def weights(q_tiles, kv_tiles, scales, out_weight):
    depth, q_cols = q_tiles.shape
    kv_cols = kv_tiles.shape[1]
    chunk = min(TILE, depth)
    return pl.pallas_call(
        weights_kernel,
        grid=(depth // chunk,),
        in_specs=[
            pl.BlockSpec((chunk, q_cols), lambda i: (i, 0)),
            pl.BlockSpec((chunk, kv_cols), lambda i: (i, 0)),
            pl.BlockSpec(scales.shape, lambda i: (0, 0)),
            IN_HBM,
        ],
        out_specs=[IN_VMEM, IN_VMEM],
        out_shape=[
            pltpu.VMEM((depth, q_cols + kv_cols), jnp.bfloat16),
            pltpu.VMEM(out_weight.shape, out_weight.dtype),
        ],
        scratch_shapes=[pltpu.SemaphoreType.DMA((4,))],
        compiler_params=PARAMS,
        cost_estimate=cost(depth * (q_cols + kv_cols), 2 * (depth * (q_cols + kv_cols) + out_weight.size)),
        name="weights",
    )(in_hbm(q_tiles), in_hbm(kv_tiles), scales, in_hbm(out_weight))


def project_kernel(turns, shards, replicas, stride, offset, behind, last, direct, place, *refs):
    count = len(turns)
    blocks, gain, weight = refs[:count], refs[count], refs[count + 1]
    before = refs[count + 2] if len(refs) == count + 6 else None
    result, total, held = refs[-3:]
    rows, width = blocks[0].shape
    columns = weight.shape[1]
    total[...] = jnp.zeros_like(total) if before is None else before[...]
    wanted = lax.rem(place[0] + replicas - behind, replicas)

    def add(block, part):
        span = pl.ds(pl.multiple_of(part * stride + offset, HEAD), width)
        squares = []
        for start in range(0, rows, STRIP):
            values = block[start:start + STRIP, :].astype(jnp.float32)
            held[start:start + STRIP, :] = (values * gain[:, span]).astype(jnp.bfloat16)
            squares.append(jnp.sum(values * values, -1, keepdims=True))
        square = jnp.broadcast_to(jnp.concatenate(squares, 0), (rows, HEAD))
        total[:, columns:] += square
        for start, size in tiles_of(columns):
            product = jnp.dot(
                held[...], weight[span, start:start + size], preferred_element_type=jnp.float32
            )
            total[:, start:start + size] += product

    for turn, block in zip(turns, blocks):
        if direct:
            add(block, lax.rem(place[1] + turn, shards // replicas))
        else:
            number = lax.rem(place[1] + shards - turn, shards)
            part = lax.div(number, replicas)
            pl.when(lax.rem(number, replicas) == wanted)(functools.partial(add, block, part))
    if last and behind:
        result[:, :columns] = total[:, :columns].astype(jnp.bfloat16)
        square = total[:, columns:]
        coarse = square.astype(jnp.bfloat16).astype(jnp.float32)
        lane = lax.broadcasted_iota(jnp.int32, square.shape, 1)
        result[:, columns:] = jnp.where(lane < HEAD // 2, coarse, square - coarse).astype(jnp.bfloat16)
    else:
        result[...] = total[...]


def project(turns, blocks, shards, replicas, stride, offset, behind, last, direct, place, gain, weight, before):
    rows, width = blocks[0].shape
    columns = weight.shape[1] + HEAD
    kind = jnp.bfloat16 if last and behind else jnp.float32
    earlier = [] if before is None else [before]
    return pl.pallas_call(
        functools.partial(project_kernel, turns, shards, replicas, stride, offset, behind, last, direct),
        in_specs=[IN_SMEM] + [IN_VMEM] * (len(blocks) + 2 + len(earlier)),
        out_specs=IN_VMEM,
        out_shape=jax.ShapeDtypeStruct((rows, columns), kind),
        scratch_shapes=[
            pltpu.VMEM((rows, columns), jnp.float32),
            pltpu.VMEM((rows, width), jnp.bfloat16),
        ],
        compiler_params=PARAMS,
        cost_estimate=cost(6 * len(blocks) * rows * width * columns, 2 * len(blocks) * width * columns),
        name="project",
    )(place, *blocks, gain, resident(weight), *earlier)


def attend_kernel(q_heads, kv_heads, features, length, own, *refs):
    received = refs[:-4]
    cosine, sine, out, cache = refs[-4:]
    rows = own.shape[0]
    group = q_heads // kv_heads

    def total(start):
        value = own[:, start:start + HEAD]
        for part in received:
            value = value + part[:, start:start + HEAD].astype(jnp.float32)
        return value

    tail = (q_heads + 2 * kv_heads) * HEAD
    square = own[:, tail:tail + 1]
    for part in received:
        pair = part[:, tail:].astype(jnp.float32)
        square = square + (pair[:, :1] + pair[:, HEAD // 2:HEAD // 2 + 1])
    factor = jnp.broadcast_to(lax.rsqrt(square / features + norm_eps), (rows, HEAD))

    def rotate(value):
        return value * cosine[...] + pltpu.roll(value, HEAD // 2, 1) * sine[...]

    row = lax.broadcasted_iota(jnp.int32, (rows, rows), 0)
    col = lax.broadcasted_iota(jnp.int32, (rows, rows), 1)
    mask = jnp.concatenate([(col <= row) & (col < length[0])] * group, 0)
    for kv_head in range(kv_heads):
        start = (q_heads + 2 * kv_head) * HEAD
        keys = rotate(total(start) * factor).astype(jnp.bfloat16)
        values = (total(start + HEAD) * factor).astype(jnp.bfloat16)
        cache[:, 2 * kv_head * HEAD:(2 * kv_head + 1) * HEAD] = keys
        cache[:, (2 * kv_head + 1) * HEAD:(2 * kv_head + 2) * HEAD] = values
        heads = range(kv_head * group, (kv_head + 1) * group)
        query = jnp.concatenate(
            [rotate(total(head * HEAD) * factor).astype(jnp.bfloat16) for head in heads], 0
        )
        scores = lax.dot_general(
            query, keys, (((1,), (1,)), ((), ())), preferred_element_type=jnp.float32
        )
        scores = jnp.where(mask, scores / jnp.sqrt(jnp.float32(HEAD)), -jnp.inf)
        expo = jnp.exp(scores - jnp.max(scores, -1, keepdims=True))
        probs = (expo / jnp.sum(expo, -1, keepdims=True)).astype(jnp.bfloat16)
        mixed = jnp.dot(probs, values, preferred_element_type=jnp.float32).astype(jnp.bfloat16)
        for number, head in enumerate(heads):
            out[:, head * HEAD:(head + 1) * HEAD] = mixed[number * rows:(number + 1) * rows, :]


def attend(own, received, length, cosine, sine, q_cols, kv_cols, features):
    rows = own.shape[0]
    return pl.pallas_call(
        functools.partial(attend_kernel, q_cols // HEAD, kv_cols // (2 * HEAD), features),
        in_specs=[IN_SMEM] + [IN_VMEM] * (3 + len(received)),
        out_specs=[IN_VMEM, IN_VMEM],
        out_shape=[
            jax.ShapeDtypeStruct((rows, q_cols), jnp.bfloat16),
            jax.ShapeDtypeStruct((rows, kv_cols), jnp.bfloat16),
        ],
        compiler_params=PARAMS,
        cost_estimate=cost(16 * rows * rows * q_cols, 6 * rows * (q_cols + kv_cols)),
        name="attend",
    )(length, own, *received, cosine, sine)


def spread_kernel(turn, shards, chunks, chunk, place, attended, weight, out):
    width = out.shape[1]
    goal = lax.rem(place[1] + turn, shards)
    for start, size in tiles_of(width):
        span = pl.ds(pl.multiple_of((goal * chunks + chunk) * width + start, HEAD), size)
        product = jnp.dot(attended[...], weight[:, span], preferred_element_type=jnp.float32)
        out[:, start:start + size] = product.astype(jnp.bfloat16)


def spread(turn, shards, chunks, chunk, place, attended, weight):
    rows, depth = attended.shape
    width = weight.shape[1] // (shards * chunks)
    return pl.pallas_call(
        functools.partial(spread_kernel, turn, shards, chunks, chunk),
        in_specs=[IN_SMEM, IN_VMEM, IN_VMEM],
        out_specs=IN_VMEM,
        out_shape=jax.ShapeDtypeStruct((rows, width), jnp.bfloat16),
        compiler_params=PARAMS,
        cost_estimate=cost(6 * rows * width * depth, 2 * depth * width),
        name="spread",
    )(place, attended, resident(weight))


def per_device(sizes, hidden_in, lengths, norm_gain, q_tiles, q_scales, kv_tiles, kv_scales, out_weight):
    replicas, sections, shards = sizes
    section = lax.axis_index("section")
    me, lane = lax.axis_index("replica"), lax.axis_index("tensor")
    rows, width = hidden_in.shape
    features = norm_gain.shape[1]
    q_tiles, kv_tiles = q_tiles[0], kv_tiles[0]
    depth, q_cols = q_tiles.shape
    kv_cols = kv_tiles.shape[1]
    per_slice = shards // replicas
    piece = width // CHUNKS
    place = jnp.stack([me, lane]).astype(jnp.int32)
    gain = lax.dynamic_slice_in_dim(norm_gain, me * depth, depth, 1)
    scales = jnp.repeat(jnp.concatenate([q_scales[0], kv_scales[0]], 1).astype(jnp.float32), BLOCK, 1)
    half = HEAD // 2
    freq = rope_base ** (-jnp.arange(half, dtype=jnp.float32) / half)
    angle = jnp.arange(rows, dtype=jnp.float32)[:, None] * freq[None, :]
    cosine = jnp.concatenate([jnp.cos(angle)] * 2, 1)
    sine = jnp.concatenate([-jnp.sin(angle), jnp.sin(angle)], 1)
    at = [section == layer for layer in range(sections)]
    scales, gain, cosine, sine, place, at, lengths, hidden_later = lax.optimization_barrier(
        (scales, gain, cosine, sine, place, at, lengths, hidden_in)
    )
    w_in, w_out = weights(q_tiles, kv_tiles, scales, out_weight[0])

    def move(value, ways, goal_of):
        pairs = []
        for source, target in ways:
            for replica in range(replicas):
                for shard in range(shards):
                    ahead, beside = goal_of(replica, shard)
                    pairs.append(
                        (
                            (replica * sections + source) * shards + shard,
                            (ahead * sections + target) * shards + beside,
                        )
                    )
        return lax.ppermute(value, AXES, pairs)

    def after(value, earlier):
        return lax.optimization_barrier((value, earlier))[0]

    def same(replica, shard):
        return replica, shard

    def shifted(turn):
        return lambda replica, shard: (replica, (shard + turn) % shards)

    def to_slice(turn):
        return lambda replica, shard: (
            shard // per_slice,
            (shard % per_slice * replicas + replica + turn) % shards,
        )

    def enter(behind, turn):
        value = hidden_in if behind else hidden_later
        rounds = {}
        for replica in range(replicas):
            for shard in range(shards):
                part, group = (shard + turn) % per_slice, shard // per_slice
                if replicas <= sections:
                    spare = sections // replicas
                    origin = (group + turn) % replicas * spare + behind % spare
                else:
                    origin = (group + turn) % sections
                origin = ((replica - behind) % replicas * sections + origin) * shards + replica * per_slice + part
                rounds.setdefault(group // sections, []).append((origin, replica * sections * shards + shard))
        return functools.reduce(jnp.add, [lax.ppermute(value, AXES, pairs) for pairs in rounds.values()])

    far_first = sorted(range(shards), key=lambda turn: -min(turn, shards - turn))
    turns = list(range(shards))
    order = list(range(1, replicas)) + [0]
    last = sections - 1
    helper = [last] * (sections - 2) + [sections - 3]
    entered = {behind: [enter(behind, turn) for turn in range(per_slice)] for behind in order}
    held, layer_out, cache_out, owed = hidden_in, hidden_in, None, None
    for layer in range(sections):
        totals, received = {}, []
        if layer == 0:
            work = [(0, True, behind) for behind in order]
        else:
            work = [(chunk, chunk == CHUNKS - 1, behind) for chunk in range(CHUNKS) for behind in order]
        for chunk, done, behind in work:
            blocks = entered[behind] if layer == 0 else pieces[chunk]
            if received:
                blocks = after(blocks, ready)
            totals[behind] = project(
                turns[:len(blocks)],
                blocks,
                shards,
                replicas,
                width,
                chunk * piece,
                behind,
                done,
                layer == 0,
                place,
                gain,
                w_in,
                totals.get(behind),
            )
            if done and behind:
                ready = totals[behind]
                goal = lambda replica, shard: ((replica - behind) % replicas, shard)
                twins = [(sect, sect) for sect in range(layer % 2, sections, 2)]
                received.append(move(ready, twins, goal))
        attended, cache = attend(totals[0], received, lengths, cosine, sine, q_cols, kv_cols, features)
        if owed is not None:
            result = move(after(owed, ready), [(helper[layer - 1], layer - 1)], same)
            layer_out = jnp.where(at[layer - 1], result, layer_out)
        if layer == last:
            value = move(after(held, ready), [(helper[last - 1], last)], same).astype(jnp.float32)
            for turn in far_first:
                partial = spread(turn, shards, 1, 0, place, attended, w_out)
                if turn:
                    partial = move(partial, [(layer, layer)], shifted(turn))
                value = value + partial.astype(jnp.float32)
            layer_out = jnp.where(at[last], value.astype(jnp.bfloat16), layer_out)
        else:
            before = held if layer < last - 1 else layer_out
            pieces, results, summands = [], [], None
            for chunk in range(CHUNKS):
                start = before[:, chunk * piece:(chunk + 1) * piece]
                given = [attended] * shards
                if chunk:
                    start = after(start, results[-1])
                    given = [after(attended, partial) for partial in summands]
                    if owed is not None:
                        given[0] = after(given[0], layer_out)
                partials = [
                    spread(turn, shards, CHUNKS, chunk, place, value, w_out)
                    for turn, value in zip(far_first, given)
                ]
                summands = [
                    move(partial, [(layer, helper[layer])], shifted(turn))
                    for turn, partial in zip(far_first, partials)
                ]
                value = start.astype(jnp.float32)
                for partial in summands:
                    value = value + partial.astype(jnp.float32)
                value = value.astype(jnp.bfloat16)
                copies = [value] * shards
                if chunk:
                    copies = [after(value, blocks) for blocks in pieces[-1]]
                ways = [(helper[layer], layer + 1)]
                pieces.append([move(copy, ways, to_slice(turn)) for turn, copy in zip(turns, copies)])
                results.append(value)
            held = jnp.concatenate(results, 1)
            owed = held
            if layer == last - 2:
                result = move(held, [(helper[layer], layer)], same)
                layer_out = jnp.where(at[layer], result, layer_out)
                owed = None
        cache_out = cache if layer == 0 else jnp.where(at[layer], cache, cache_out)
        if layer < last:
            layer_out, cache_out = lax.optimization_barrier((layer_out, cache_out))
    return layer_out[None], cache_out[None]


def solution(mesh):
    sizes = tuple(mesh.shape[axis] for axis in AXES)
    in_specs = (
        P("replica", "tensor"),
        P("replica"),
        P("section", None),
        P("section", "replica", "tensor"),
        P("section", "replica", "tensor"),
        P("section", "replica", "tensor"),
        P("section", "replica", "tensor"),
        P("section", "tensor", None),
    )
    out_specs = (P("section", "replica", "tensor"), P("section", "replica", "tensor"))
    return jax.shard_map(
        functools.partial(per_device, sizes),
        mesh=mesh,
        in_specs=in_specs,
        out_specs=out_specs,
        check_vma=False,
    )
```

```python
import functools

import jax
import jax.numpy as jnp
from jax import lax
from jax.experimental import pallas as pl
from jax.experimental.pallas import tpu as pltpu
from jax.sharding import PartitionSpec as P

HEAD = 128
BLOCK = 128
STRIP = 16
TILE = 512
CHUNKS = 2

rope_base = 1000000.0
norm_eps = 1e-06

AXES = ("replica", "section", "tensor")
PARAMS = pltpu.CompilerParams(vmem_limit_bytes=8 * 1024 * 1024)
IN_VMEM = pl.BlockSpec(memory_space=pltpu.VMEM)
IN_SMEM = pl.BlockSpec(memory_space=pltpu.SMEM)
IN_HBM = pl.BlockSpec(memory_space=pl.ANY)


def cost(flops, moved):
    return pl.CostEstimate(flops=flops, bytes_accessed=moved, transcendentals=0)


def resident(value):
    return pltpu.with_memory_space_constraint(value, pltpu.VMEM)


def in_hbm(value):
    return pltpu.with_memory_space_constraint(value, pltpu.HBM)


def tiles_of(columns):
    return [(start, min(TILE, columns - start)) for start in range(0, columns, TILE)]


def weights_kernel(q_tile, kv_tile, scale, source, out, target, done):
    step = pl.program_id(0)
    q_cols = q_tile.shape[1]
    chunk = q_tile.shape[0]
    parts = done.shape[0]
    depth = source.shape[0] // parts
    copies = []
    for part in range(parts):
        span = pl.ds(part * depth, depth)
        copies.append(pltpu.make_async_copy(source.at[span], target.at[span], done.at[part]))

    @pl.when(step == 0)
    def _():
        for copy in copies:
            copy.start()

    for number in range(chunk // BLOCK):
        rows = pl.ds(number * BLOCK, BLOCK)
        goal = pl.ds(pl.multiple_of(step * chunk + number * BLOCK, BLOCK), BLOCK)
        line = scale[pl.ds(step * (chunk // BLOCK) + number, 1), :]
        for tile, left in ((q_tile, 0), (kv_tile, q_cols)):
            width = tile.shape[1]
            factor = jnp.broadcast_to(line[:, left:left + width], (BLOCK, width))
            value = tile[rows, :].astype(jnp.float32) * factor
            out[goal, left:left + width] = value.astype(jnp.bfloat16)

    @pl.when(step == pl.num_programs(0) - 1)
    def _():
        for copy in copies:
            copy.wait()


def weights(q_tiles, kv_tiles, scales, out_weight):
    depth, q_cols = q_tiles.shape
    kv_cols = kv_tiles.shape[1]
    chunk = min(TILE, depth)
    return pl.pallas_call(
        weights_kernel,
        grid=(depth // chunk,),
        in_specs=[
            pl.BlockSpec((chunk, q_cols), lambda i: (i, 0)),
            pl.BlockSpec((chunk, kv_cols), lambda i: (i, 0)),
            pl.BlockSpec(scales.shape, lambda i: (0, 0)),
            IN_HBM,
        ],
        out_specs=[IN_VMEM, IN_VMEM],
        out_shape=[
            pltpu.VMEM((depth, q_cols + kv_cols), jnp.bfloat16),
            pltpu.VMEM(out_weight.shape, out_weight.dtype),
        ],
        scratch_shapes=[pltpu.SemaphoreType.DMA((4,))],
        compiler_params=PARAMS,
        cost_estimate=cost(depth * (q_cols + kv_cols), 2 * (depth * (q_cols + kv_cols) + out_weight.size)),
        name="weights",
    )(in_hbm(q_tiles), in_hbm(kv_tiles), scales, in_hbm(out_weight))


def project_kernel(turns, shards, replicas, stride, offset, behind, last, direct, place, *refs):
    count = len(turns)
    blocks, gain, weight = refs[:count], refs[count], refs[count + 1]
    before = refs[count + 2] if len(refs) == count + 6 else None
    result, total, held = refs[-3:]
    rows, width = blocks[0].shape
    columns = weight.shape[1]
    total[...] = jnp.zeros_like(total) if before is None else before[...]
    wanted = lax.rem(place[0] + replicas - behind, replicas)

    def add(block, part):
        span = pl.ds(pl.multiple_of(part * stride + offset, HEAD), width)
        squares = []
        for start in range(0, rows, STRIP):
            values = block[start:start + STRIP, :].astype(jnp.float32)
            held[start:start + STRIP, :] = (values * gain[:, span]).astype(jnp.bfloat16)
            squares.append(jnp.sum(values * values, -1, keepdims=True))
        square = jnp.broadcast_to(jnp.concatenate(squares, 0), (rows, HEAD))
        total[:, columns:] += square
        for start, size in tiles_of(columns):
            product = jnp.dot(
                held[...], weight[span, start:start + size], preferred_element_type=jnp.float32
            )
            total[:, start:start + size] += product

    for turn, block in zip(turns, blocks):
        if direct:
            add(block, lax.rem(place[1] + turn, shards // replicas))
        else:
            number = lax.rem(place[1] + shards - turn, shards)
            part = lax.div(number, replicas)
            pl.when(lax.rem(number, replicas) == wanted)(functools.partial(add, block, part))
    if last and behind:
        result[:, :columns] = total[:, :columns].astype(jnp.bfloat16)
        square = total[:, columns:]
        coarse = square.astype(jnp.bfloat16).astype(jnp.float32)
        lane = lax.broadcasted_iota(jnp.int32, square.shape, 1)
        result[:, columns:] = jnp.where(lane < HEAD // 2, coarse, square - coarse).astype(jnp.bfloat16)
    else:
        result[...] = total[...]


def project(turns, blocks, shards, replicas, stride, offset, behind, last, direct, place, gain, weight, before):
    rows, width = blocks[0].shape
    columns = weight.shape[1] + HEAD
    kind = jnp.bfloat16 if last and behind else jnp.float32
    earlier = [] if before is None else [before]
    return pl.pallas_call(
        functools.partial(project_kernel, turns, shards, replicas, stride, offset, behind, last, direct),
        in_specs=[IN_SMEM] + [IN_VMEM] * (len(blocks) + 2 + len(earlier)),
        out_specs=IN_VMEM,
        out_shape=jax.ShapeDtypeStruct((rows, columns), kind),
        scratch_shapes=[
            pltpu.VMEM((rows, columns), jnp.float32),
            pltpu.VMEM((rows, width), jnp.bfloat16),
        ],
        compiler_params=PARAMS,
        cost_estimate=cost(6 * len(blocks) * rows * width * columns, 2 * len(blocks) * width * columns),
        name="project",
    )(place, *blocks, gain, resident(weight), *earlier)


def attend_kernel(q_heads, kv_heads, features, length, own, *refs):
    received = refs[:-4]
    cosine, sine, out, cache = refs[-4:]
    rows = own.shape[0]
    group = q_heads // kv_heads

    def total(start):
        value = own[:, start:start + HEAD]
        for part in received:
            value = value + part[:, start:start + HEAD].astype(jnp.float32)
        return value

    tail = (q_heads + 2 * kv_heads) * HEAD
    square = own[:, tail:tail + 1]
    for part in received:
        pair = part[:, tail:].astype(jnp.float32)
        square = square + (pair[:, :1] + pair[:, HEAD // 2:HEAD // 2 + 1])
    factor = jnp.broadcast_to(lax.rsqrt(square / features + norm_eps), (rows, HEAD))

    def rotate(value):
        return value * cosine[...] + pltpu.roll(value, HEAD // 2, 1) * sine[...]

    row = lax.broadcasted_iota(jnp.int32, (rows, rows), 0)
    col = lax.broadcasted_iota(jnp.int32, (rows, rows), 1)
    mask = jnp.concatenate([(col <= row) & (col < length[0])] * group, 0)
    for kv_head in range(kv_heads):
        start = (q_heads + 2 * kv_head) * HEAD
        keys = rotate(total(start) * factor).astype(jnp.bfloat16)
        values = (total(start + HEAD) * factor).astype(jnp.bfloat16)
        cache[:, 2 * kv_head * HEAD:(2 * kv_head + 1) * HEAD] = keys
        cache[:, (2 * kv_head + 1) * HEAD:(2 * kv_head + 2) * HEAD] = values
        heads = range(kv_head * group, (kv_head + 1) * group)
        query = jnp.concatenate(
            [rotate(total(head * HEAD) * factor).astype(jnp.bfloat16) for head in heads], 0
        )
        scores = lax.dot_general(
            query, keys, (((1,), (1,)), ((), ())), preferred_element_type=jnp.float32
        )
        scores = jnp.where(mask, scores / jnp.sqrt(jnp.float32(HEAD)), -jnp.inf)
        expo = jnp.exp(scores - jnp.max(scores, -1, keepdims=True))
        probs = (expo / jnp.sum(expo, -1, keepdims=True)).astype(jnp.bfloat16)
        mixed = jnp.dot(probs, values, preferred_element_type=jnp.float32).astype(jnp.bfloat16)
        for number, head in enumerate(heads):
            out[:, head * HEAD:(head + 1) * HEAD] = mixed[number * rows:(number + 1) * rows, :]


def attend(own, received, length, cosine, sine, q_cols, kv_cols, features):
    rows = own.shape[0]
    return pl.pallas_call(
        functools.partial(attend_kernel, q_cols // HEAD, kv_cols // (2 * HEAD), features),
        in_specs=[IN_SMEM] + [IN_VMEM] * (3 + len(received)),
        out_specs=[IN_VMEM, IN_VMEM],
        out_shape=[
            jax.ShapeDtypeStruct((rows, q_cols), jnp.bfloat16),
            jax.ShapeDtypeStruct((rows, kv_cols), jnp.bfloat16),
        ],
        compiler_params=PARAMS,
        cost_estimate=cost(16 * rows * rows * q_cols, 6 * rows * (q_cols + kv_cols)),
        name="attend",
    )(length, own, *received, cosine, sine)


def spread_kernel(turn, shards, chunks, chunk, place, attended, weight, out):
    width = out.shape[1]
    goal = lax.rem(place[1] + turn, shards)
    for start, size in tiles_of(width):
        span = pl.ds(pl.multiple_of((goal * chunks + chunk) * width + start, HEAD), size)
        product = jnp.dot(attended[...], weight[:, span], preferred_element_type=jnp.float32)
        out[:, start:start + size] = product.astype(jnp.bfloat16)


def spread(turn, shards, chunks, chunk, place, attended, weight):
    rows, depth = attended.shape
    width = weight.shape[1] // (shards * chunks)
    return pl.pallas_call(
        functools.partial(spread_kernel, turn, shards, chunks, chunk),
        in_specs=[IN_SMEM, IN_VMEM, IN_VMEM],
        out_specs=IN_VMEM,
        out_shape=jax.ShapeDtypeStruct((rows, width), jnp.bfloat16),
        compiler_params=PARAMS,
        cost_estimate=cost(6 * rows * width * depth, 2 * depth * width),
        name="spread",
    )(place, attended, resident(weight))


def per_device(sizes, hidden_in, lengths, norm_gain, q_tiles, q_scales, kv_tiles, kv_scales, out_weight):
    replicas, sections, shards = sizes
    section = lax.axis_index("section")
    me, lane = lax.axis_index("replica"), lax.axis_index("tensor")
    rows, width = hidden_in.shape
    features = norm_gain.shape[1]
    q_tiles, kv_tiles = q_tiles[0], kv_tiles[0]
    depth, q_cols = q_tiles.shape
    kv_cols = kv_tiles.shape[1]
    per_slice = shards // replicas
    piece = width // CHUNKS
    place = jnp.stack([me, lane]).astype(jnp.int32)
    gain = lax.dynamic_slice_in_dim(norm_gain, me * depth, depth, 1)
    scales = jnp.repeat(jnp.concatenate([q_scales[0], kv_scales[0]], 1).astype(jnp.float32), BLOCK, 1)
    half = HEAD // 2
    freq = rope_base ** (-jnp.arange(half, dtype=jnp.float32) / half)
    angle = jnp.arange(rows, dtype=jnp.float32)[:, None] * freq[None, :]
    cosine = jnp.concatenate([jnp.cos(angle)] * 2, 1)
    sine = jnp.concatenate([-jnp.sin(angle), jnp.sin(angle)], 1)
    at = [section == layer for layer in range(sections)]
    scales, gain, cosine, sine, place, at, lengths, hidden_later = lax.optimization_barrier(
        (scales, gain, cosine, sine, place, at, lengths, hidden_in)
    )
    w_in, w_out = weights(q_tiles, kv_tiles, scales, out_weight[0])

    def move(value, ways, goal_of):
        pairs = []
        for source, target in ways:
            for replica in range(replicas):
                for shard in range(shards):
                    ahead, beside = goal_of(replica, shard)
                    pairs.append(
                        (
                            (replica * sections + source) * shards + shard,
                            (ahead * sections + target) * shards + beside,
                        )
                    )
        return lax.ppermute(value, AXES, pairs)

    def after(value, earlier):
        return lax.optimization_barrier((value, earlier))[0]

    def same(replica, shard):
        return replica, shard

    def shifted(turn):
        return lambda replica, shard: (replica, (shard + turn) % shards)

    def to_slice(turn):
        return lambda replica, shard: (
            shard // per_slice,
            (shard % per_slice * replicas + replica + turn) % shards,
        )

    def enter(behind, turn):
        value = hidden_in if behind else hidden_later
        rounds = {}
        for replica in range(replicas):
            for shard in range(shards):
                part, group = (shard + turn) % per_slice, shard // per_slice
                if replicas <= sections:
                    spare = sections // replicas
                    origin = (group + turn) % replicas * spare + behind % spare
                else:
                    origin = (group + turn) % sections
                origin = ((replica - behind) % replicas * sections + origin) * shards + replica * per_slice + part
                rounds.setdefault(group // sections, []).append((origin, replica * sections * shards + shard))
        return functools.reduce(jnp.add, [lax.ppermute(value, AXES, pairs) for pairs in rounds.values()])

    far_first = sorted(range(shards), key=lambda turn: -min(turn, shards - turn))
    turns = list(range(shards))
    sum_order, gather_order = far_first, turns[::-1]
    order = list(range(1, replicas)) + [0]
    last = sections - 1
    helper = [last] * (sections - 2) + [sections - 3]
    entered = {behind: [enter(behind, turn) for turn in range(per_slice)] for behind in order}
    held, layer_out, cache_out, owed = hidden_in, hidden_in, None, None
    for layer in range(sections):
        totals, received = {}, []
        if layer == 0:
            work = [(0, True, behind) for behind in order]
        else:
            work = [(chunk, chunk == CHUNKS - 1, behind) for chunk in range(CHUNKS) for behind in order]
        for chunk, done, behind in work:
            blocks = entered[behind] if layer == 0 else pieces[chunk]
            if received:
                blocks = after(blocks, ready)
            totals[behind] = project(
                gather_order if layer else turns[:len(blocks)],
                blocks,
                shards,
                replicas,
                width,
                chunk * piece,
                behind,
                done,
                layer == 0,
                place,
                gain,
                w_in,
                totals.get(behind),
            )
            if done and behind:
                ready = totals[behind]
                goal = lambda replica, shard: ((replica - behind) % replicas, shard)
                twins = [(sect, sect) for sect in range(layer % 2, sections, 2)]
                received.append(move(ready, twins, goal))
        attended, cache = attend(totals[0], received, lengths, cosine, sine, q_cols, kv_cols, features)
        if owed is not None:
            result = move(after(owed, ready), [(helper[layer - 1], layer - 1)], same)
            layer_out = jnp.where(at[layer - 1], result, layer_out)
        if layer == last:
            residual = move(after(held, ready), [(helper[last - 1], last)], same)
            value = residual.astype(jnp.float32)
            for turn in far_first:
                given = attended if turn == far_first[0] else after(attended, residual)
                partial = spread(turn, shards, 1, 0, place, given, w_out)
                if turn:
                    partial = move(partial, [(layer, layer)], shifted(turn))
                value = value + partial.astype(jnp.float32)
            layer_out = jnp.where(at[last], value.astype(jnp.bfloat16), layer_out)
        else:
            before = held if layer < last - 1 else layer_out
            pieces, results, summands = [], [], None
            for chunk in range(CHUNKS):
                start = before[:, chunk * piece:(chunk + 1) * piece]
                given = [attended] * shards
                if chunk:
                    start = after(start, results[-1])
                    given = [after(attended, partial) for partial in summands]
                    if owed is not None:
                        given[0] = after(given[0], layer_out)
                partials = [
                    spread(turn, shards, CHUNKS, chunk, place, value, w_out)
                    for turn, value in zip(sum_order, given)
                ]
                summands = [
                    move(partial, [(layer, helper[layer])], shifted(turn))
                    for turn, partial in zip(sum_order, partials)
                ]
                value = start.astype(jnp.float32)
                for partial in summands:
                    value = value + partial.astype(jnp.float32)
                value = value.astype(jnp.bfloat16)
                copies = [value] * shards
                if chunk:
                    copies = [after(value, blocks) for blocks in pieces[-1]]
                ways = [(helper[layer], layer + 1)]
                pieces.append([move(copy, ways, to_slice(turn)) for turn, copy in zip(gather_order, copies)])
                results.append(value)
            held = jnp.concatenate(results, 1)
            owed = held
            if layer == last - 2:
                result = move(held, [(helper[layer], layer)], same)
                layer_out = jnp.where(at[layer], result, layer_out)
                owed = None
        cache_out = cache if layer == 0 else jnp.where(at[layer], cache, cache_out)
        if layer < last:
            layer_out, cache_out = lax.optimization_barrier((layer_out, cache_out))
    return layer_out[None], cache_out[None]


def solution(mesh):
    sizes = tuple(mesh.shape[axis] for axis in AXES)
    in_specs = (
        P("replica", "tensor"),
        P("replica"),
        P("section", None),
        P("section", "replica", "tensor"),
        P("section", "replica", "tensor"),
        P("section", "replica", "tensor"),
        P("section", "replica", "tensor"),
        P("section", "tensor", None),
    )
    out_specs = (P("section", "replica", "tensor"), P("section", "replica", "tensor"))
    return jax.shard_map(
        functools.partial(per_device, sizes),
        mesh=mesh,
        in_specs=in_specs,
        out_specs=out_specs,
        check_vma=False,
    )
```

```python
import functools

import jax
import jax.numpy as jnp
from jax import lax
from jax.experimental import pallas as pl
from jax.experimental.pallas import tpu as pltpu
from jax.sharding import PartitionSpec as P

HEAD = 128
BLOCK = 128
STRIP = 16
TILE = 512
CHUNKS = 2

rope_base = 1000000.0
norm_eps = 1e-06

AXES = ("replica", "section", "tensor")
PARAMS = pltpu.CompilerParams(vmem_limit_bytes=8 * 1024 * 1024)
IN_VMEM = pl.BlockSpec(memory_space=pltpu.VMEM)
IN_SMEM = pl.BlockSpec(memory_space=pltpu.SMEM)
IN_HBM = pl.BlockSpec(memory_space=pl.ANY)


def cost(flops, moved):
    return pl.CostEstimate(flops=flops, bytes_accessed=moved, transcendentals=0)


def resident(value):
    return pltpu.with_memory_space_constraint(value, pltpu.VMEM)


def in_hbm(value):
    return pltpu.with_memory_space_constraint(value, pltpu.HBM)


def tiles_of(columns):
    return [(start, min(TILE, columns - start)) for start in range(0, columns, TILE)]


def weights_kernel(q_tile, kv_tile, scale, source, out, target, done):
    step = pl.program_id(0)
    q_cols = q_tile.shape[1]
    chunk = q_tile.shape[0]
    parts = done.shape[0]
    depth = source.shape[0] // parts
    copies = []
    for part in range(parts):
        span = pl.ds(part * depth, depth)
        copies.append(pltpu.make_async_copy(source.at[span], target.at[span], done.at[part]))

    @pl.when(step == 0)
    def _():
        for copy in copies:
            copy.start()

    for number in range(chunk // BLOCK):
        rows = pl.ds(number * BLOCK, BLOCK)
        goal = pl.ds(pl.multiple_of(step * chunk + number * BLOCK, BLOCK), BLOCK)
        line = scale[pl.ds(step * (chunk // BLOCK) + number, 1), :]
        for tile, left in ((q_tile, 0), (kv_tile, q_cols)):
            width = tile.shape[1]
            factor = jnp.broadcast_to(line[:, left:left + width], (BLOCK, width))
            value = tile[rows, :].astype(jnp.float32) * factor
            out[goal, left:left + width] = value.astype(jnp.bfloat16)

    @pl.when(step == pl.num_programs(0) - 1)
    def _():
        for copy in copies:
            copy.wait()


def weights(q_tiles, kv_tiles, scales, out_weight):
    depth, q_cols = q_tiles.shape
    kv_cols = kv_tiles.shape[1]
    chunk = min(2 * TILE, depth)
    return pl.pallas_call(
        weights_kernel,
        grid=(depth // chunk,),
        in_specs=[
            pl.BlockSpec((chunk, q_cols), lambda i: (i, 0)),
            pl.BlockSpec((chunk, kv_cols), lambda i: (i, 0)),
            pl.BlockSpec(scales.shape, lambda i: (0, 0)),
            IN_HBM,
        ],
        out_specs=[IN_VMEM, IN_VMEM],
        out_shape=[
            pltpu.VMEM((depth, q_cols + kv_cols), jnp.bfloat16),
            pltpu.VMEM(out_weight.shape, out_weight.dtype),
        ],
        scratch_shapes=[pltpu.SemaphoreType.DMA((4,))],
        compiler_params=pltpu.CompilerParams(vmem_limit_bytes=12 * 1024 * 1024),
        cost_estimate=cost(depth * (q_cols + kv_cols), 2 * (depth * (q_cols + kv_cols) + out_weight.size)),
        name="weights",
    )(in_hbm(q_tiles), in_hbm(kv_tiles), scales, in_hbm(out_weight))


def project_kernel(turns, shards, replicas, stride, offset, behind, last, direct, place, *refs):
    count = len(turns)
    blocks, gain, weight = refs[:count], refs[count], refs[count + 1]
    before = refs[count + 2] if len(refs) == count + 6 else None
    result, total, held = refs[-3:]
    rows, width = blocks[0].shape
    columns = weight.shape[1]
    total[...] = jnp.zeros_like(total) if before is None else before[...]
    wanted = lax.rem(place[0] + replicas - behind, replicas)

    def add(block, part):
        span = pl.ds(pl.multiple_of(part * stride + offset, HEAD), width)
        squares = []
        for start in range(0, rows, STRIP):
            values = block[start:start + STRIP, :].astype(jnp.float32)
            held[start:start + STRIP, :] = (values * gain[:, span]).astype(jnp.bfloat16)
            squares.append(jnp.sum(values * values, -1, keepdims=True))
        square = jnp.broadcast_to(jnp.concatenate(squares, 0), (rows, HEAD))
        total[:, columns:] += square
        for start, size in tiles_of(columns):
            product = jnp.dot(
                held[...], weight[span, start:start + size], preferred_element_type=jnp.float32
            )
            total[:, start:start + size] += product

    for turn, block in zip(turns, blocks):
        if direct:
            add(block, lax.rem(place[1] + turn, shards // replicas))
        else:
            number = lax.rem(place[1] + shards - turn, shards)
            part = lax.div(number, replicas)
            pl.when(lax.rem(number, replicas) == wanted)(functools.partial(add, block, part))
    if last and behind:
        result[:, :columns] = total[:, :columns].astype(jnp.bfloat16)
        square = total[:, columns:]
        coarse = square.astype(jnp.bfloat16).astype(jnp.float32)
        lane = lax.broadcasted_iota(jnp.int32, square.shape, 1)
        result[:, columns:] = jnp.where(lane < HEAD // 2, coarse, square - coarse).astype(jnp.bfloat16)
    else:
        result[...] = total[...]


def project(turns, blocks, shards, replicas, stride, offset, behind, last, direct, place, gain, weight, before):
    rows, width = blocks[0].shape
    columns = weight.shape[1] + HEAD
    kind = jnp.bfloat16 if last and behind else jnp.float32
    earlier = [] if before is None else [before]
    return pl.pallas_call(
        functools.partial(project_kernel, turns, shards, replicas, stride, offset, behind, last, direct),
        in_specs=[IN_SMEM] + [IN_VMEM] * (len(blocks) + 2 + len(earlier)),
        out_specs=IN_VMEM,
        out_shape=jax.ShapeDtypeStruct((rows, columns), kind),
        scratch_shapes=[
            pltpu.VMEM((rows, columns), jnp.float32),
            pltpu.VMEM((rows, width), jnp.bfloat16),
        ],
        compiler_params=PARAMS,
        cost_estimate=cost(6 * len(blocks) * rows * width * columns, 2 * len(blocks) * width * columns),
        name="project",
    )(place, *blocks, gain, resident(weight), *earlier)


def attend_kernel(q_heads, kv_heads, features, length, own, *refs):
    received = refs[:-4]
    cosine, sine, out, cache = refs[-4:]
    rows = own.shape[0]
    group = q_heads // kv_heads

    def total(start):
        value = own[:, start:start + HEAD]
        for part in received:
            value = value + part[:, start:start + HEAD].astype(jnp.float32)
        return value

    tail = (q_heads + 2 * kv_heads) * HEAD
    square = own[:, tail:tail + 1]
    for part in received:
        pair = part[:, tail:].astype(jnp.float32)
        square = square + (pair[:, :1] + pair[:, HEAD // 2:HEAD // 2 + 1])
    factor = jnp.broadcast_to(lax.rsqrt(square / features + norm_eps), (rows, HEAD))

    def rotate(value):
        return value * cosine[...] + pltpu.roll(value, HEAD // 2, 1) * sine[...]

    row = lax.broadcasted_iota(jnp.int32, (rows, rows), 0)
    col = lax.broadcasted_iota(jnp.int32, (rows, rows), 1)
    mask = jnp.concatenate([(col <= row) & (col < length[0])] * group, 0)
    for kv_head in range(kv_heads):
        start = (q_heads + 2 * kv_head) * HEAD
        keys = rotate(total(start) * factor).astype(jnp.bfloat16)
        values = (total(start + HEAD) * factor).astype(jnp.bfloat16)
        cache[:, 2 * kv_head * HEAD:(2 * kv_head + 1) * HEAD] = keys
        cache[:, (2 * kv_head + 1) * HEAD:(2 * kv_head + 2) * HEAD] = values
        heads = range(kv_head * group, (kv_head + 1) * group)
        query = jnp.concatenate(
            [rotate(total(head * HEAD) * factor).astype(jnp.bfloat16) for head in heads], 0
        )
        scores = lax.dot_general(
            query, keys, (((1,), (1,)), ((), ())), preferred_element_type=jnp.float32
        )
        scores = jnp.where(mask, scores / jnp.sqrt(jnp.float32(HEAD)), -jnp.inf)
        expo = jnp.exp(scores - jnp.max(scores, -1, keepdims=True))
        probs = (expo / jnp.sum(expo, -1, keepdims=True)).astype(jnp.bfloat16)
        mixed = jnp.dot(probs, values, preferred_element_type=jnp.float32).astype(jnp.bfloat16)
        for number, head in enumerate(heads):
            out[:, head * HEAD:(head + 1) * HEAD] = mixed[number * rows:(number + 1) * rows, :]


def attend(own, received, length, cosine, sine, q_cols, kv_cols, features):
    rows = own.shape[0]
    return pl.pallas_call(
        functools.partial(attend_kernel, q_cols // HEAD, kv_cols // (2 * HEAD), features),
        in_specs=[IN_SMEM] + [IN_VMEM] * (3 + len(received)),
        out_specs=[IN_VMEM, IN_VMEM],
        out_shape=[
            jax.ShapeDtypeStruct((rows, q_cols), jnp.bfloat16),
            jax.ShapeDtypeStruct((rows, kv_cols), jnp.bfloat16),
        ],
        compiler_params=PARAMS,
        cost_estimate=cost(16 * rows * rows * q_cols, 6 * rows * (q_cols + kv_cols)),
        name="attend",
    )(length, own, *received, cosine, sine)


def spread_kernel(turn, shards, chunks, chunk, place, attended, weight, out):
    width = out.shape[1]
    goal = lax.rem(place[1] + turn, shards)
    for start, size in tiles_of(width):
        span = pl.ds(pl.multiple_of((goal * chunks + chunk) * width + start, HEAD), size)
        product = jnp.dot(attended[...], weight[:, span], preferred_element_type=jnp.float32)
        out[:, start:start + size] = product.astype(jnp.bfloat16)


def spread(turn, shards, chunks, chunk, place, attended, weight):
    rows, depth = attended.shape
    width = weight.shape[1] // (shards * chunks)
    return pl.pallas_call(
        functools.partial(spread_kernel, turn, shards, chunks, chunk),
        in_specs=[IN_SMEM, IN_VMEM, IN_VMEM],
        out_specs=IN_VMEM,
        out_shape=jax.ShapeDtypeStruct((rows, width), jnp.bfloat16),
        compiler_params=PARAMS,
        cost_estimate=cost(6 * rows * width * depth, 2 * depth * width),
        name="spread",
    )(place, attended, resident(weight))


def per_device(sizes, hidden_in, lengths, norm_gain, q_tiles, q_scales, kv_tiles, kv_scales, out_weight):
    replicas, sections, shards = sizes
    section = lax.axis_index("section")
    me, lane = lax.axis_index("replica"), lax.axis_index("tensor")
    rows, width = hidden_in.shape
    features = norm_gain.shape[1]
    q_tiles, kv_tiles = q_tiles[0], kv_tiles[0]
    depth, q_cols = q_tiles.shape
    kv_cols = kv_tiles.shape[1]
    per_slice = shards // replicas
    piece = width // CHUNKS
    place = jnp.stack([me, lane]).astype(jnp.int32)
    gain = lax.dynamic_slice_in_dim(norm_gain, me * depth, depth, 1)
    scales = jnp.repeat(jnp.concatenate([q_scales[0], kv_scales[0]], 1).astype(jnp.float32), BLOCK, 1)
    half = HEAD // 2
    freq = rope_base ** (-jnp.arange(half, dtype=jnp.float32) / half)
    angle = jnp.arange(rows, dtype=jnp.float32)[:, None] * freq[None, :]
    cosine = jnp.concatenate([jnp.cos(angle)] * 2, 1)
    sine = jnp.concatenate([-jnp.sin(angle), jnp.sin(angle)], 1)
    at = [section == layer for layer in range(sections)]
    scales, gain, cosine, sine, place, at, lengths, hidden_later = lax.optimization_barrier(
        (scales, gain, cosine, sine, place, at, lengths, hidden_in)
    )
    w_in, w_out = weights(q_tiles, kv_tiles, scales, out_weight[0])

    def move(value, ways, goal_of):
        pairs = []
        for source, target in ways:
            for replica in range(replicas):
                for shard in range(shards):
                    ahead, beside = goal_of(replica, shard)
                    pairs.append(
                        (
                            (replica * sections + source) * shards + shard,
                            (ahead * sections + target) * shards + beside,
                        )
                    )
        return lax.ppermute(value, AXES, pairs)

    def after(value, earlier):
        return lax.optimization_barrier((value, earlier))[0]

    def same(replica, shard):
        return replica, shard

    def shifted(turn):
        return lambda replica, shard: (replica, (shard + turn) % shards)

    def to_slice(turn):
        return lambda replica, shard: (
            shard // per_slice,
            (shard % per_slice * replicas + replica + turn) % shards,
        )

    def enter(behind, turn):
        value = hidden_in if behind else hidden_later
        rounds = {}
        for replica in range(replicas):
            for shard in range(shards):
                part, group = (shard + turn) % per_slice, shard // per_slice
                if replicas <= sections:
                    spare = sections // replicas
                    origin = (group + turn) % replicas * spare + behind % spare
                else:
                    origin = (group + turn) % sections
                origin = ((replica - behind) % replicas * sections + origin) * shards + replica * per_slice + part
                rounds.setdefault(group // sections, []).append((origin, replica * sections * shards + shard))
        return functools.reduce(jnp.add, [lax.ppermute(value, AXES, pairs) for pairs in rounds.values()])

    far_first = sorted(range(shards), key=lambda turn: -min(turn, shards - turn))
    turns = list(range(shards))
    sum_order, gather_order = far_first, turns[::-1]
    order = list(range(1, replicas)) + [0]
    last = sections - 1
    helper = [last] * (sections - 2) + [sections - 3]
    entered = {behind: [enter(behind, turn) for turn in range(per_slice)] for behind in order}
    held, layer_out, cache_out, owed = hidden_in, hidden_in, None, None
    for layer in range(sections):
        totals, received = {}, []
        if layer == 0:
            work = [(0, True, behind) for behind in order]
        else:
            work = [(chunk, chunk == CHUNKS - 1, behind) for chunk in range(CHUNKS) for behind in order]
        for chunk, done, behind in work:
            blocks = entered[behind] if layer == 0 else pieces[chunk]
            if received:
                blocks = after(blocks, ready)
            totals[behind] = project(
                gather_order if layer else turns[:len(blocks)],
                blocks,
                shards,
                replicas,
                width,
                chunk * piece,
                behind,
                done,
                layer == 0,
                place,
                gain,
                w_in,
                totals.get(behind),
            )
            if done and behind:
                ready = totals[behind]
                goal = lambda replica, shard: ((replica - behind) % replicas, shard)
                twins = [(sect, sect) for sect in range(layer % 2, sections, 2)]
                received.append(move(ready, twins, goal))
        attended, cache = attend(totals[0], received, lengths, cosine, sine, q_cols, kv_cols, features)
        if owed is not None:
            result = move(after(owed, ready), [(helper[layer - 1], layer - 1)], same)
            layer_out = jnp.where(at[layer - 1], result, layer_out)
        if layer == last:
            residual = move(after(held, ready), [(helper[last - 1], last)], same)
            value = residual.astype(jnp.float32)
            for turn in far_first:
                given = attended if turn == far_first[0] else after(attended, residual)
                partial = spread(turn, shards, 1, 0, place, given, w_out)
                if turn:
                    partial = move(partial, [(layer, layer)], shifted(turn))
                value = value + partial.astype(jnp.float32)
            layer_out = jnp.where(at[last], value.astype(jnp.bfloat16), layer_out)
        else:
            before = held if layer < last - 1 else layer_out
            pieces, results, summands = [], [], None
            for chunk in range(CHUNKS):
                start = before[:, chunk * piece:(chunk + 1) * piece]
                given = [attended] * shards
                if chunk:
                    start = after(start, results[-1])
                    given = [after(attended, partial) for partial in summands]
                    if owed is not None:
                        given[0] = after(given[0], layer_out)
                partials = [
                    spread(turn, shards, CHUNKS, chunk, place, value, w_out)
                    for turn, value in zip(sum_order, given)
                ]
                summands = [
                    move(partial, [(layer, helper[layer])], shifted(turn))
                    for turn, partial in zip(sum_order, partials)
                ]
                value = start.astype(jnp.float32)
                for partial in summands:
                    value = value + partial.astype(jnp.float32)
                value = value.astype(jnp.bfloat16)
                copies = [value] * shards
                if chunk:
                    copies = [after(value, blocks) for blocks in pieces[-1]]
                ways = [(helper[layer], layer + 1)]
                pieces.append([move(copy, ways, to_slice(turn)) for turn, copy in zip(gather_order, copies)])
                results.append(value)
            held = jnp.concatenate(results, 1)
            owed = held
            if layer == last - 2:
                result = move(held, [(helper[layer], layer)], same)
                layer_out = jnp.where(at[layer], result, layer_out)
                owed = None
        cache_out = cache if layer == 0 else jnp.where(at[layer], cache, cache_out)
        if layer < last:
            layer_out, cache_out = lax.optimization_barrier((layer_out, cache_out))
    return layer_out[None], cache_out[None]


def solution(mesh):
    sizes = tuple(mesh.shape[axis] for axis in AXES)
    in_specs = (
        P("replica", "tensor"),
        P("replica"),
        P("section", None),
        P("section", "replica", "tensor"),
        P("section", "replica", "tensor"),
        P("section", "replica", "tensor"),
        P("section", "replica", "tensor"),
        P("section", "tensor", None),
    )
    out_specs = (P("section", "replica", "tensor"), P("section", "replica", "tensor"))
    return jax.shard_map(
        functools.partial(per_device, sizes),
        mesh=mesh,
        in_specs=in_specs,
        out_specs=out_specs,
        check_vma=False,
    )
```

```python
import functools

import jax
import jax.numpy as jnp
from jax import lax
from jax.experimental import pallas as pl
from jax.experimental.pallas import tpu as pltpu
from jax.sharding import PartitionSpec as P

HEAD = 128
BLOCK = 128
STRIP = 16
TILE = 1024
CHUNKS = 2

rope_base = 1000000.0
norm_eps = 1e-06

AXES = ("replica", "section", "tensor")
PARAMS = pltpu.CompilerParams(vmem_limit_bytes=8 * 1024 * 1024)
IN_VMEM = pl.BlockSpec(memory_space=pltpu.VMEM)
IN_SMEM = pl.BlockSpec(memory_space=pltpu.SMEM)
IN_HBM = pl.BlockSpec(memory_space=pl.ANY)


def cost(flops, moved):
    return pl.CostEstimate(flops=flops, bytes_accessed=moved, transcendentals=0)


def resident(value):
    return pltpu.with_memory_space_constraint(value, pltpu.VMEM)


def in_hbm(value):
    return pltpu.with_memory_space_constraint(value, pltpu.HBM)


def tiles_of(columns):
    return [(start, min(TILE, columns - start)) for start in range(0, columns, TILE)]


def weights_kernel(q_tile, kv_tile, scale, source, out, target, done):
    step = pl.program_id(0)
    q_cols = q_tile.shape[1]
    chunk = q_tile.shape[0]
    parts = done.shape[0]
    depth = source.shape[0] // parts
    copies = []
    for part in range(parts):
        span = pl.ds(part * depth, depth)
        copies.append(pltpu.make_async_copy(source.at[span], target.at[span], done.at[part]))

    @pl.when(step == 0)
    def _():
        for copy in copies:
            copy.start()

    for number in range(chunk // BLOCK):
        rows = pl.ds(number * BLOCK, BLOCK)
        goal = pl.ds(pl.multiple_of(step * chunk + number * BLOCK, BLOCK), BLOCK)
        line = scale[pl.ds(step * (chunk // BLOCK) + number, 1), :]
        for tile, left in ((q_tile, 0), (kv_tile, q_cols)):
            width = tile.shape[1]
            factor = jnp.broadcast_to(line[:, left:left + width], (BLOCK, width))
            value = tile[rows, :].astype(jnp.float32) * factor
            out[goal, left:left + width] = value.astype(jnp.bfloat16)

    @pl.when(step == pl.num_programs(0) - 1)
    def _():
        for copy in copies:
            copy.wait()


def weights(q_tiles, kv_tiles, scales, out_weight):
    depth, q_cols = q_tiles.shape
    kv_cols = kv_tiles.shape[1]
    chunk = min(TILE, depth)
    return pl.pallas_call(
        weights_kernel,
        grid=(depth // chunk,),
        in_specs=[
            pl.BlockSpec((chunk, q_cols), lambda i: (i, 0)),
            pl.BlockSpec((chunk, kv_cols), lambda i: (i, 0)),
            pl.BlockSpec(scales.shape, lambda i: (0, 0)),
            IN_HBM,
        ],
        out_specs=[IN_VMEM, IN_VMEM],
        out_shape=[
            pltpu.VMEM((depth, q_cols + kv_cols), jnp.bfloat16),
            pltpu.VMEM(out_weight.shape, out_weight.dtype),
        ],
        scratch_shapes=[pltpu.SemaphoreType.DMA((4,))],
        compiler_params=pltpu.CompilerParams(vmem_limit_bytes=12 * 1024 * 1024),
        cost_estimate=cost(depth * (q_cols + kv_cols), 2 * (depth * (q_cols + kv_cols) + out_weight.size)),
        name="weights",
    )(in_hbm(q_tiles), in_hbm(kv_tiles), scales, in_hbm(out_weight))


def project_kernel(turns, shards, replicas, stride, offset, behind, last, direct, place, *refs):
    count = len(turns)
    blocks, gain, weight = refs[:count], refs[count], refs[count + 1]
    before = refs[count + 2] if len(refs) == count + 6 else None
    result, total, held = refs[-3:]
    rows, width = blocks[0].shape
    columns = weight.shape[1]
    total[...] = jnp.zeros_like(total) if before is None else before[...]
    wanted = lax.rem(place[0] + replicas - behind, replicas)

    def add(block, part):
        span = pl.ds(pl.multiple_of(part * stride + offset, HEAD), width)
        squares = []
        for start in range(0, rows, STRIP):
            values = block[start:start + STRIP, :].astype(jnp.float32)
            held[start:start + STRIP, :] = (values * gain[:, span]).astype(jnp.bfloat16)
            squares.append(jnp.sum(values * values, -1, keepdims=True))
        square = jnp.broadcast_to(jnp.concatenate(squares, 0), (rows, HEAD))
        total[:, columns:] += square
        for start, size in tiles_of(columns):
            product = jnp.dot(
                held[...], weight[span, start:start + size], preferred_element_type=jnp.float32
            )
            total[:, start:start + size] += product

    for turn, block in zip(turns, blocks):
        if direct:
            add(block, lax.rem(place[1] + turn, shards // replicas))
        else:
            number = lax.rem(place[1] + shards - turn, shards)
            part = lax.div(number, replicas)
            pl.when(lax.rem(number, replicas) == wanted)(functools.partial(add, block, part))
    if last and behind:
        result[:, :columns] = total[:, :columns].astype(jnp.bfloat16)
        square = total[:, columns:]
        coarse = square.astype(jnp.bfloat16).astype(jnp.float32)
        lane = lax.broadcasted_iota(jnp.int32, square.shape, 1)
        result[:, columns:] = jnp.where(lane < HEAD // 2, coarse, square - coarse).astype(jnp.bfloat16)
    else:
        result[...] = total[...]


def project(turns, blocks, shards, replicas, stride, offset, behind, last, direct, place, gain, weight, before):
    rows, width = blocks[0].shape
    columns = weight.shape[1] + HEAD
    kind = jnp.bfloat16 if last and behind else jnp.float32
    earlier = [] if before is None else [before]
    return pl.pallas_call(
        functools.partial(project_kernel, turns, shards, replicas, stride, offset, behind, last, direct),
        in_specs=[IN_SMEM] + [IN_VMEM] * (len(blocks) + 2 + len(earlier)),
        out_specs=IN_VMEM,
        out_shape=jax.ShapeDtypeStruct((rows, columns), kind),
        scratch_shapes=[
            pltpu.VMEM((rows, columns), jnp.float32),
            pltpu.VMEM((rows, width), jnp.bfloat16),
        ],
        compiler_params=PARAMS,
        cost_estimate=cost(6 * len(blocks) * rows * width * columns, 2 * len(blocks) * width * columns),
        name="project",
    )(place, *blocks, gain, resident(weight), *earlier)


def attend_kernel(q_heads, kv_heads, features, length, own, *refs):
    received = refs[:-4]
    cosine, sine, out, cache = refs[-4:]
    rows = own.shape[0]
    group = q_heads // kv_heads

    def total(start):
        value = own[:, start:start + HEAD]
        for part in received:
            value = value + part[:, start:start + HEAD].astype(jnp.float32)
        return value

    tail = (q_heads + 2 * kv_heads) * HEAD
    square = own[:, tail:tail + 1]
    for part in received:
        pair = part[:, tail:].astype(jnp.float32)
        square = square + (pair[:, :1] + pair[:, HEAD // 2:HEAD // 2 + 1])
    factor = jnp.broadcast_to(lax.rsqrt(square / features + norm_eps), (rows, HEAD))

    def rotate(value):
        return value * cosine[...] + pltpu.roll(value, HEAD // 2, 1) * sine[...]

    row = lax.broadcasted_iota(jnp.int32, (rows, rows), 0)
    col = lax.broadcasted_iota(jnp.int32, (rows, rows), 1)
    mask = jnp.concatenate([(col <= row) & (col < length[0])] * group, 0)
    for kv_head in range(kv_heads):
        start = (q_heads + 2 * kv_head) * HEAD
        keys = rotate(total(start) * factor).astype(jnp.bfloat16)
        values = (total(start + HEAD) * factor).astype(jnp.bfloat16)
        cache[:, 2 * kv_head * HEAD:(2 * kv_head + 1) * HEAD] = keys
        cache[:, (2 * kv_head + 1) * HEAD:(2 * kv_head + 2) * HEAD] = values
        heads = range(kv_head * group, (kv_head + 1) * group)
        query = jnp.concatenate(
            [rotate(total(head * HEAD) * factor).astype(jnp.bfloat16) for head in heads], 0
        )
        scores = lax.dot_general(
            query, keys, (((1,), (1,)), ((), ())), preferred_element_type=jnp.float32
        )
        scores = jnp.where(mask, scores / jnp.sqrt(jnp.float32(HEAD)), -jnp.inf)
        expo = jnp.exp(scores - jnp.max(scores, -1, keepdims=True))
        probs = (expo / jnp.sum(expo, -1, keepdims=True)).astype(jnp.bfloat16)
        mixed = jnp.dot(probs, values, preferred_element_type=jnp.float32).astype(jnp.bfloat16)
        for number, head in enumerate(heads):
            out[:, head * HEAD:(head + 1) * HEAD] = mixed[number * rows:(number + 1) * rows, :]


def attend(own, received, length, cosine, sine, q_cols, kv_cols, features):
    rows = own.shape[0]
    return pl.pallas_call(
        functools.partial(attend_kernel, q_cols // HEAD, kv_cols // (2 * HEAD), features),
        in_specs=[IN_SMEM] + [IN_VMEM] * (3 + len(received)),
        out_specs=[IN_VMEM, IN_VMEM],
        out_shape=[
            jax.ShapeDtypeStruct((rows, q_cols), jnp.bfloat16),
            jax.ShapeDtypeStruct((rows, kv_cols), jnp.bfloat16),
        ],
        compiler_params=PARAMS,
        cost_estimate=cost(16 * rows * rows * q_cols, 6 * rows * (q_cols + kv_cols)),
        name="attend",
    )(length, own, *received, cosine, sine)


def spread_kernel(turn, shards, chunks, chunk, place, attended, weight, out):
    width = out.shape[1]
    goal = lax.rem(place[1] + turn, shards)
    for start, size in tiles_of(width):
        span = pl.ds(pl.multiple_of((goal * chunks + chunk) * width + start, HEAD), size)
        product = jnp.dot(attended[...], weight[:, span], preferred_element_type=jnp.float32)
        out[:, start:start + size] = product.astype(jnp.bfloat16)


def spread(turn, shards, chunks, chunk, place, attended, weight):
    rows, depth = attended.shape
    width = weight.shape[1] // (shards * chunks)
    return pl.pallas_call(
        functools.partial(spread_kernel, turn, shards, chunks, chunk),
        in_specs=[IN_SMEM, IN_VMEM, IN_VMEM],
        out_specs=IN_VMEM,
        out_shape=jax.ShapeDtypeStruct((rows, width), jnp.bfloat16),
        compiler_params=PARAMS,
        cost_estimate=cost(6 * rows * width * depth, 2 * depth * width),
        name="spread",
    )(place, attended, resident(weight))


def per_device(sizes, hidden_in, lengths, norm_gain, q_tiles, q_scales, kv_tiles, kv_scales, out_weight):
    replicas, sections, shards = sizes
    section = lax.axis_index("section")
    me, lane = lax.axis_index("replica"), lax.axis_index("tensor")
    rows, width = hidden_in.shape
    features = norm_gain.shape[1]
    q_tiles, kv_tiles = q_tiles[0], kv_tiles[0]
    depth, q_cols = q_tiles.shape
    kv_cols = kv_tiles.shape[1]
    per_slice = shards // replicas
    piece = width // CHUNKS
    place = jnp.stack([me, lane]).astype(jnp.int32)
    gain = lax.dynamic_slice_in_dim(norm_gain, me * depth, depth, 1)
    scales = jnp.repeat(jnp.concatenate([q_scales[0], kv_scales[0]], 1).astype(jnp.float32), BLOCK, 1)
    half = HEAD // 2
    freq = rope_base ** (-jnp.arange(half, dtype=jnp.float32) / half)
    angle = jnp.arange(rows, dtype=jnp.float32)[:, None] * freq[None, :]
    cosine = jnp.concatenate([jnp.cos(angle)] * 2, 1)
    sine = jnp.concatenate([-jnp.sin(angle), jnp.sin(angle)], 1)
    at = [section == layer for layer in range(sections)]
    scales, gain, cosine, sine, place, at, lengths, hidden_later = lax.optimization_barrier(
        (scales, gain, cosine, sine, place, at, lengths, hidden_in)
    )
    w_in, w_out = weights(q_tiles, kv_tiles, scales, out_weight[0])

    def move(value, ways, goal_of):
        pairs = []
        for source, target in ways:
            for replica in range(replicas):
                for shard in range(shards):
                    ahead, beside = goal_of(replica, shard)
                    pairs.append(
                        (
                            (replica * sections + source) * shards + shard,
                            (ahead * sections + target) * shards + beside,
                        )
                    )
        return lax.ppermute(value, AXES, pairs)

    def after(value, earlier):
        return lax.optimization_barrier((value, earlier))[0]

    def same(replica, shard):
        return replica, shard

    def shifted(turn):
        return lambda replica, shard: (replica, (shard + turn) % shards)

    def to_slice(turn):
        return lambda replica, shard: (
            shard // per_slice,
            (shard % per_slice * replicas + replica + turn) % shards,
        )

    def enter(behind, turn):
        value = hidden_in if behind else hidden_later
        rounds = {}
        for replica in range(replicas):
            for shard in range(shards):
                part, group = (shard + turn) % per_slice, shard // per_slice
                if replicas <= sections:
                    spare = sections // replicas
                    origin = (group + turn) % replicas * spare + behind % spare
                else:
                    origin = (group + turn) % sections
                origin = ((replica - behind) % replicas * sections + origin) * shards + replica * per_slice + part
                rounds.setdefault(group // sections, []).append((origin, replica * sections * shards + shard))
        return functools.reduce(jnp.add, [lax.ppermute(value, AXES, pairs) for pairs in rounds.values()])

    far_first = sorted(range(shards), key=lambda turn: -min(turn, shards - turn))
    turns = list(range(shards))
    sum_order, gather_order = far_first, turns[::-1]
    order = list(range(1, replicas)) + [0]
    last = sections - 1
    helper = [last] * (sections - 2) + [sections - 3]
    entered = {behind: [enter(behind, turn) for turn in range(per_slice)] for behind in order}
    held, layer_out, cache_out, owed = hidden_in, hidden_in, None, None
    for layer in range(sections):
        totals, received = {}, []
        if layer == 0:
            work = [(0, True, behind) for behind in order]
        else:
            work = [(chunk, chunk == CHUNKS - 1, behind) for chunk in range(CHUNKS) for behind in order]
        for chunk, done, behind in work:
            blocks = entered[behind] if layer == 0 else pieces[chunk]
            if received:
                blocks = after(blocks, ready)
            totals[behind] = project(
                gather_order if layer else turns[:len(blocks)],
                blocks,
                shards,
                replicas,
                width,
                chunk * piece,
                behind,
                done,
                layer == 0,
                place,
                gain,
                w_in,
                totals.get(behind),
            )
            if done and behind:
                ready = totals[behind]
                goal = lambda replica, shard: ((replica - behind) % replicas, shard)
                twins = [(sect, sect) for sect in range(layer % 2, sections, 2)]
                received.append(move(ready, twins, goal))
        attended, cache = attend(totals[0], received, lengths, cosine, sine, q_cols, kv_cols, features)
        if owed is not None:
            result = move(after(owed, ready), [(helper[layer - 1], layer - 1)], same)
            layer_out = jnp.where(at[layer - 1], result, layer_out)
        if layer == last:
            residual = move(after(held, ready), [(helper[last - 1], last)], same)
            value = residual.astype(jnp.float32)
            for turn in far_first:
                given = attended if turn == far_first[0] else after(attended, residual)
                partial = spread(turn, shards, 1, 0, place, given, w_out)
                if turn:
                    partial = move(partial, [(layer, layer)], shifted(turn))
                value = value + partial.astype(jnp.float32)
            layer_out = jnp.where(at[last], value.astype(jnp.bfloat16), layer_out)
        else:
            before = held if layer < last - 1 else layer_out
            pieces, results, summands = [], [], None
            for chunk in range(CHUNKS):
                start = before[:, chunk * piece:(chunk + 1) * piece]
                given = [attended] * shards
                if chunk:
                    start = after(start, results[-1])
                    given = [after(attended, partial) for partial in summands]
                    if owed is not None:
                        given[0] = after(given[0], layer_out)
                partials = [
                    spread(turn, shards, CHUNKS, chunk, place, value, w_out)
                    for turn, value in zip(sum_order, given)
                ]
                summands = [
                    move(partial, [(layer, helper[layer])], shifted(turn))
                    for turn, partial in zip(sum_order, partials)
                ]
                value = start.astype(jnp.float32)
                for partial in summands:
                    value = value + partial.astype(jnp.float32)
                value = value.astype(jnp.bfloat16)
                copies = [value] * shards
                if chunk:
                    copies = [after(value, blocks) for blocks in pieces[-1]]
                ways = [(helper[layer], layer + 1)]
                pieces.append([move(copy, ways, to_slice(turn)) for turn, copy in zip(gather_order, copies)])
                results.append(value)
            held = jnp.concatenate(results, 1)
            owed = held
            if layer == last - 2:
                result = move(held, [(helper[layer], layer)], same)
                layer_out = jnp.where(at[layer], result, layer_out)
                owed = None
        cache_out = cache if layer == 0 else jnp.where(at[layer], cache, cache_out)
        if layer < last:
            layer_out, cache_out = lax.optimization_barrier((layer_out, cache_out))
    return layer_out[None], cache_out[None]


def solution(mesh):
    sizes = tuple(mesh.shape[axis] for axis in AXES)
    in_specs = (
        P("replica", "tensor"),
        P("replica"),
        P("section", None),
        P("section", "replica", "tensor"),
        P("section", "replica", "tensor"),
        P("section", "replica", "tensor"),
        P("section", "replica", "tensor"),
        P("section", "tensor", None),
    )
    out_specs = (P("section", "replica", "tensor"), P("section", "replica", "tensor"))
    return jax.shard_map(
        functools.partial(per_device, sizes),
        mesh=mesh,
        in_specs=in_specs,
        out_specs=out_specs,
        check_vma=False,
    )
```
